32 devices in a mesh: fsdp: 4 (over z), ctx: 2 (over core), tp: 4 (over y, x).
Axes of the slice: x: 2, y: 2, z: 4, core: 2. Of those that a mesh axis runs over, the one named last changes fastest.
Arguments:
- token_ids: int32 [4, 1024], P('fsdp', 'ctx'), may hold values from 0 to 1023
- masked: int32 [4, 1024], P('fsdp', 'ctx'), may hold values from 0 to 1, as said below
- tile_slot: int32 [36], replicated, may hold values from 0 to 47, as said below
- tile_master: float32 [48, 768, 768], P('fsdp', 'tp'), may hold values from -0.21875 to 0.21875
- tile_first: float32 [48, 768, 768], P('fsdp', 'tp'), may hold values from -0.0009765625 to 0.0009765625
- tile_second: float32 [48, 768, 768], P('fsdp', 'tp'), may hold values from 2.4414062e-09 to 9.765625e-09
- embedding: float32 [768, 2025], P('fsdp'), may hold values from -0.3125 to 0.3125
- embed_first: float32 [768, 2025], P('fsdp'), may hold values from -0.0009765625 to 0.0009765625
- embed_second: float32 [768, 2025], P('fsdp'), may hold values from 2.4414062e-09 to 9.765625e-09
- position_table: float32 [768, 1024], P('fsdp'), may hold values from -0.3125 to 0.3125
- position_first: float32 [768, 1024], P('fsdp'), may hold values from -0.00030517578 to 0.00030517578
- position_second: float32 [768, 1024], P('fsdp'), may hold values from 2.384186e-10 to 9.536744e-10
- norm_params: float32 [2, 7, 768], P(None, None, 'fsdp')
- norm_first: float32 [2, 7, 768], P(None, None, 'fsdp'), may hold values from -0.0009765625 to 0.0009765625
- norm_second: float32 [2, 7, 768], P(None, None, 'fsdp'), may hold values from 2.4414062e-09 to 9.765625e-09
- head_bias: float32 [2025], replicated, may hold values from -3 to 3
- bias_first: float32 [2025], replicated, may hold values from -0.0009765625 to 0.0009765625
- bias_second: float32 [2025], replicated, may hold values from 2.4414062e-09 to 9.765625e-09
Outputs:
- loss_value: float32 [], replicated
- tile_new: float32 [48, 768, 768], P('fsdp', 'tp')
- tile_first_new: float32 [48, 768, 768], P('fsdp', 'tp')
- tile_second_new: float32 [48, 768, 768], P('fsdp', 'tp')
- embedding_new: float32 [768, 2025], P('fsdp')
- embed_first_new: float32 [768, 2025], P('fsdp')
- embed_second_new: float32 [768, 2025], P('fsdp')
- position_new: float32 [768, 1024], P('fsdp')
- position_first_new: float32 [768, 1024], P('fsdp')
- position_second_new: float32 [768, 1024], P('fsdp')
- norm_new: float32 [2, 7, 768], P(None, None, 'fsdp')
- norm_first_new: float32 [2, 7, 768], P(None, None, 'fsdp')
- norm_second_new: float32 [2, 7, 768], P(None, None, 'fsdp')
- bias_new: float32 [2025], replicated
- bias_first_new: float32 [2025], replicated
- bias_second_new: float32 [2025], replicated
The draws below stay inside these ranges and needn't reach their ends.
Inputs may be any that keep to these rules, and one draw needn't show every extreme that they name: The last place of every image is masked. `tile_slot`: tile t belongs to layer t // 12, in the order q, k, v, output, four input tiles, four output tiles. The values are distinct; slot s belongs to index s // 12 of fsdp, and some index holds 12 tiles.
All inputs are finite; a program needn't handle non-finite values.
Results may differ from the reference program's by a relative error of at most 0.025.
The reference program's roundings to bfloat16 on the way count: a program that leaves them out, or rounds other values in their place, can miss the bound.
Values may be sent and summed in bfloat16 or wider, within the bound.
No kernel may reach another device: no remote copies, remote signals or barrier semaphores. Data moves between devices by JAX's collectives and lax.ppermute only.
A program may use at most 320 MiB of HBM per device.

```python
import math
import jax
import jax.numpy as jnp
from jax import lax

D = 768
HEADS = 16
HEAD_DIM = 48
VOCAB = 2025
CODES = 1024
SEQ = 1024
LAYERS = 3
STEP = 10
IMAGES = 4
TILES = 36
NORMS = 7
CAP = 12
SLOTS = 48


def draw_masked(key, part):
    draws = jax.random.randint(key, (IMAGES, SEQ), 0, 2000)
    image_at = lax.broadcasted_iota(jnp.int32, (IMAGES, SEQ), 0)
    place_at = lax.broadcasted_iota(jnp.int32, (IMAGES, SEQ), 1)
    limit = (150 + 300 * image_at // max(IMAGES - 1, 1)) * (1 + 2 * (place_at >= SEQ // 2).astype(jnp.int32))
    return jnp.where((draws < limit) | (place_at == SEQ - 1), 1, 0).astype(jnp.int32)


def draw_tile_slot(key, part):
    order_key = jax.random.fold_in(key, 11)
    owner_key = jax.random.fold_in(key, 12)
    tile_key = jax.random.fold_in(key, 13)
    shuffled = jax.random.permutation(order_key, SLOTS)
    ranking = jnp.zeros((SLOTS,), jnp.int32).at[shuffled].set(jnp.arange(SLOTS, dtype=jnp.int32))
    full_owner = jax.random.randint(owner_key, (), 0, SLOTS // CAP)
    owner_of = jnp.arange(SLOTS, dtype=jnp.int32) // CAP
    score_rank = jnp.where(owner_of == full_owner, ranking - SLOTS, ranking)
    chosen = jnp.argsort(score_rank)[:TILES]
    return chosen[jax.random.permutation(tile_key, TILES)].astype(jnp.int32)


def draw_norm_params(key, part):
    gain_key = jax.random.fold_in(key, 21)
    shift_key = jax.random.fold_in(key, 22)
    gains = 1.0 + 0.2 * jax.random.normal(gain_key, (NORMS, D), jnp.float32)
    shifts = 0.2 * jax.random.normal(shift_key, (NORMS, D), jnp.float32)
    return jnp.stack([gains, shifts])


def with_ends(drawn, rng, least, high):
    index_at = [jax.random.randint(jax.random.fold_in(rng, axis), (), 0, length) for axis, length in enumerate(drawn.shape)]
    widest = drawn.shape.index(max(drawn.shape))
    next_to = index_at[:widest] + [(index_at[widest] + 1) % drawn.shape[widest]] + index_at[widest + 1:]
    return drawn.at[tuple(index_at)].set(least).at[tuple(next_to)].set(high)


def levels(stream_key, dims, split, low, top_value):
    level = 1.0
    for dim, blocks in split:
        heights = jax.random.uniform(jax.random.fold_in(jax.random.fold_in(stream_key, 6), dim), (blocks,), jnp.float32, low / len(split), top_value / len(split))
        level = level * jnp.repeat(jnp.exp(heights), dims[dim] // blocks).reshape((-1,) + (1,) * (len(dims) - 1 - dim))
    return level


def noise(own_key, dims, deviation, most, cuts=(), held_as=jnp.bfloat16):
    result = deviation * jax.random.normal(own_key, dims, jnp.float32)
    if cuts:
        result = result * levels(own_key, dims, cuts, -0.22, 0.18)
    return jnp.clip(result, -most, most).astype(held_as)


def setup_inputs(seed: int = 0) -> dict:
    key_list = jax.random.split(jax.random.key(seed), 19)
    token_ids = with_ends(jax.random.randint(key_list[0], (IMAGES, SEQ), 0, CODES), jax.random.fold_in(key_list[0], 1), 0, CODES - 1).astype(jnp.int32)
    masked = draw_masked(jax.random.fold_in(key_list[18], 71), 0)
    tile_slot = draw_tile_slot(jax.random.fold_in(key_list[18], 71), 0)
    tile_master = noise(key_list[3], (SLOTS, D, D), D ** -0.5, 0.21875, ((0, 4), (1, 4)), jnp.float32)
    tile_first = noise(key_list[4], (SLOTS, D, D), (0.011 * (IMAGES * SEQ) ** -0.5), 0.0009765625, ((0, 4), (1, 4)), jnp.float32)
    tile_second = jnp.clip(jnp.exp(math.log(9.765624753299562e-09) - 1.3862944 * jax.random.uniform(key_list[5], (SLOTS, D, D), jnp.float32) ** levels(key_list[5], (SLOTS, D, D), ((0, 4), (1, 4)), -0.2, 0.2)), 2.4414061883248905e-09, 9.765624753299562e-09)
    embedding = noise(key_list[6], (D, VOCAB), 0.05, 0.3125, ((0, 4),), jnp.float32)
    embed_first = noise(key_list[7], (D, VOCAB), (0.011 * (IMAGES * SEQ) ** -0.5), 0.0009765625, ((0, 4),), jnp.float32)
    embed_second = jnp.clip(jnp.exp(math.log(9.765624753299562e-09) - 1.3862944 * jax.random.uniform(key_list[8], (D, VOCAB), jnp.float32) ** levels(key_list[8], (D, VOCAB), ((0, 4),), -0.2, 0.2)), 2.4414061883248905e-09, 9.765624753299562e-09)
    position_table = noise(key_list[9], (D, SEQ), 0.05, 0.3125, ((0, 4),), jnp.float32)
    position_first = noise(key_list[10], (D, SEQ), (0.11 * IMAGES ** -0.5 / SEQ), 0.00030517578, ((0, 4),), jnp.float32)
    position_second = jnp.clip(jnp.exp(math.log(9.536743617033494e-10) - 1.3862944 * jax.random.uniform(key_list[11], (D, SEQ), jnp.float32) ** levels(key_list[11], (D, SEQ), ((0, 4),), -0.2, 0.2)), 2.3841859042583735e-10, 9.536743617033494e-10)
    norm_params = draw_norm_params(jax.random.fold_in(key_list[18], 71), 0)
    norm_first = noise(key_list[13], (2, NORMS, D), (0.011 * (IMAGES * SEQ) ** -0.5), 0.0009765625, ((2, 4),), jnp.float32)
    norm_second = jnp.clip(jnp.exp(math.log(9.765624753299562e-09) - 1.3862944 * jax.random.uniform(key_list[14], (2, NORMS, D), jnp.float32) ** levels(key_list[14], (2, NORMS, D), ((2, 4),), -0.2, 0.2)), 2.4414061883248905e-09, 9.765624753299562e-09)
    head_bias = noise(key_list[15], (VOCAB,), 0.5, 3.0, (), jnp.float32)
    bias_first = noise(key_list[16], (VOCAB,), (0.011 * (IMAGES * SEQ) ** -0.5), 0.0009765625, (), jnp.float32)
    bias_second = jnp.clip(jnp.exp(jax.random.uniform(key_list[17], (VOCAB,), jnp.float32, math.log(2.4414061883248905e-09), math.log(9.765624753299562e-09))), 2.4414061883248905e-09, 9.765624753299562e-09)
    return dict(token_ids=token_ids, masked=masked, tile_slot=tile_slot, tile_master=tile_master, tile_first=tile_first, tile_second=tile_second, embedding=embedding, embed_first=embed_first, embed_second=embed_second, position_table=position_table, position_first=position_first, position_second=position_second, norm_params=norm_params, norm_first=norm_first, norm_second=norm_second, head_bias=head_bias, bias_first=bias_first, bias_second=bias_second)


@jax.custom_vjp
def low(v):
    return lax.optimization_barrier(v.astype(jnp.bfloat16)).astype(jnp.float32)

@jax.custom_vjp
def low_back(v):
    return v

def low_keep(v):
    return (low(v), None)

def low_pass(kept, grad):
    return (grad,)

def back_keep(v):
    return (v, None)

def back_low(kept, grad):
    return (low(grad),)
low.defvjp(low_keep, low_pass)
low_back.defvjp(back_keep, back_low)
highest = lax.Precision.HIGHEST
norm_eps = 1e-05
beta_first = 0.9
beta_second = 0.999
learn_rate = 0.05
small_rate = 0.5
weight_decay = 0.01
adam_eps = 1e-08

def matmul_high(left, right):
    return jnp.dot(left, right, precision=highest, preferred_element_type=jnp.float32)

def layer_norm(stream, gain, shift):
    centered = stream - lax.optimization_barrier(jnp.mean(stream, -1, keepdims=True))
    return centered * lax.rsqrt(lax.optimization_barrier(jnp.mean(centered * centered, -1, keepdims=True)) + norm_eps) * gain + shift

def forward(params, id_block, mask_block, total_count):
    tile_full, embed_table, position_rows, norm_rows, bias_row = params
    tile_full = low(tile_full)
    embed_table = low(embed_table).T
    position_rows = low(position_rows).T
    norm_rows = low(norm_rows)
    images = id_block.shape[0]
    inputs = jnp.where(mask_block == 1, VOCAB - 1, id_block)
    stream = (embed_table[inputs] + position_rows[None]).reshape(images * SEQ, D)
    score_scale = HEAD_DIM ** (-0.5)
    heads_shape = (images, SEQ, HEADS, HEAD_DIM)
    for layer_idx in range(LAYERS):
        layer_tiles = tile_full[12 * layer_idx:12 * layer_idx + 12]
        normed = low(layer_norm(stream, norm_rows[0, 2 * layer_idx], norm_rows[1, 2 * layer_idx]))
        queries = low(low_back(matmul_high(normed, layer_tiles[0].T))).reshape(heads_shape)
        key_rows = low(low_back(matmul_high(normed, layer_tiles[1].T))).reshape(heads_shape)
        value_rows = low(low_back(matmul_high(normed, layer_tiles[2].T))).reshape(heads_shape)
        scores = low_back(jnp.einsum('gqhc,gkhc->ghqk', queries, key_rows, precision=highest) * score_scale)
        attn_weights = low(jax.nn.softmax(scores, -1))
        mixed_heads = jnp.einsum('ghqk,gkhc->gqhc', attn_weights, value_rows, precision=highest).reshape(images * SEQ, D)
        mixed_heads = low(low_back(mixed_heads))
        stream = stream + low_back(matmul_high(mixed_heads, layer_tiles[3]))
        normed_mlp = low(layer_norm(stream, norm_rows[0, 2 * layer_idx + 1], norm_rows[1, 2 * layer_idx + 1]))
        hidden_in = jnp.concatenate([layer_tiles[4], layer_tiles[5], layer_tiles[6], layer_tiles[7]], 0).T
        hidden_out = jnp.concatenate([layer_tiles[8], layer_tiles[9], layer_tiles[10], layer_tiles[11]], 0)
        pre_gelu = low_back(matmul_high(normed_mlp, hidden_in))
        activation = low(jax.nn.gelu(pre_gelu, approximate=False))
        stream = stream + low_back(matmul_high(activation, hidden_out))
    final_normed = low(layer_norm(stream, norm_rows[0, 2 * LAYERS], norm_rows[1, 2 * LAYERS]))
    logits = low_back(matmul_high(final_normed, embed_table.T) + bias_row)
    log_total = jax.nn.logsumexp(logits, -1)
    picked = jnp.take_along_axis(logits, id_block.reshape(-1, 1), 1)[:, 0]
    return jnp.sum((log_total - picked) * mask_block.reshape(-1).astype(jnp.float32)) / total_count

def adamw_update(weight, moment_one, moment_two, gradient, rate):
    moment_one = beta_first * moment_one + (1.0 - beta_first) * gradient
    moment_two = beta_second * moment_two + (1.0 - beta_second) * gradient * gradient
    first_hat = moment_one / (1.0 - beta_first ** STEP)
    second_hat = moment_two / (1.0 - beta_second ** STEP)
    weight = weight - rate * (first_hat / (jnp.sqrt(second_hat) + adam_eps) + weight_decay * weight)
    return (weight, moment_one, moment_two)

def reference(token_ids, masked, tile_slot, tile_master, tile_first, tile_second, embedding, embed_first, embed_second, position_table, position_first, position_second, norm_params, norm_first, norm_second, head_bias, bias_first, bias_second):
    total_count = jnp.sum(masked).astype(jnp.float32)
    params = (tile_master[tile_slot], embedding, position_table, norm_params, head_bias)
    group_size = math.gcd(4, IMAGES)
    id_blocks = token_ids.reshape(IMAGES // group_size, group_size, SEQ)
    mask_blocks = masked.reshape(IMAGES // group_size, group_size, SEQ)

    def accumulate(running, blocks):
        block_loss, pullback = jax.vjp(lambda values: forward(values, blocks[0], blocks[1], total_count), params)
        gradients = pullback(jnp.ones((), jnp.float32))[0]
        return ((running[0] + block_loss, jax.tree.map(jnp.add, running[1], gradients)), None)
    zeros_start = jax.tree.map(jnp.zeros_like, params)
    (loss_value, gradients), _ = lax.scan(accumulate, (jnp.zeros((), jnp.float32), zeros_start), (id_blocks, mask_blocks))
    slot_grads = jnp.zeros_like(tile_master).at[tile_slot].set(gradients[0])
    in_use = jnp.zeros((tile_master.shape[0], 1, 1), jnp.float32).at[tile_slot].set(1.0) > 0.5
    tile_upd = adamw_update(tile_master, tile_first, tile_second, slot_grads, learn_rate)
    tile_new = jnp.where(in_use, tile_upd[0], tile_master)
    tile_one = jnp.where(in_use, tile_upd[1], tile_first)
    tile_two = jnp.where(in_use, tile_upd[2], tile_second)
    embed_upd = adamw_update(embedding, embed_first, embed_second, gradients[1], learn_rate)
    position_upd = adamw_update(position_table, position_first, position_second, gradients[2], learn_rate)
    norm_upd = adamw_update(norm_params, norm_first, norm_second, gradients[3], small_rate)
    bias_upd = adamw_update(head_bias, bias_first, bias_second, gradients[4], small_rate)
    return (loss_value, tile_new, tile_one, tile_two, embed_upd[0], embed_upd[1], embed_upd[2], position_upd[0], position_upd[1], position_upd[2], norm_upd[0], norm_upd[1], norm_upd[2], bias_upd[0], bias_upd[1], bias_upd[2])
```

```python
import functools

import jax
import jax.numpy as jnp
from jax import lax
from jax.experimental import pallas as pl
from jax.experimental.pallas import tpu as pltpu
from jax.sharding import PartitionSpec as P

HEAD_DIM = 48
VOCAB = 2025
LAYERS = 3
STEP = 10
TILES = 36
BLOCK = 256
GROUP = 2
LAG = 2

norm_eps = 1e-05
beta_first = 0.9
beta_second = 0.999
learn_rate = 0.05
small_rate = 0.5
weight_decay = 0.01
adam_eps = 1e-08

bf16 = jnp.bfloat16
f32 = jnp.float32
FLIP_X = [(i, i ^ 1) for i in range(4)]
FLIP_Y = [(i, i ^ 2) for i in range(4)]
FLIP_CORE = [(0, 1), (1, 0)]


def over_x(v):
    return lax.ppermute(v, "tp", FLIP_X)


def over_y(v):
    return lax.ppermute(v, "tp", FLIP_Y)


def over_core(v):
    return lax.ppermute(v, "ctx", FLIP_CORE)


def dot(left, right, dims):
    return lax.dot_general(left, right, (dims, ((), ())), preferred_element_type=f32)


def norm_parts(stream, gain, shift):
    centered = stream - jnp.mean(stream, -1, keepdims=True)
    inverse = lax.rsqrt(jnp.mean(centered * centered, -1, keepdims=True) + norm_eps)
    normal_hat = centered * inverse
    return (normal_hat * gain + shift, normal_hat, inverse)


def norm_back(gradient, normal_hat, inverse, gain):
    scaled = gradient * gain
    return inverse * (
        scaled
        - jnp.mean(scaled, -1, keepdims=True)
        - normal_hat * jnp.mean(scaled * normal_hat, -1, keepdims=True)
    )


def gelu_slope(pre_gelu):
    return (
        0.5 * (1.0 + lax.erf(pre_gelu * 0.7071067811865476))
        + pre_gelu * jnp.exp(-0.5 * pre_gelu * pre_gelu) * 0.3989422804014327
    )


def sum_over_x(partial):
    mine = partial.astype(bf16)
    return mine.astype(f32) + over_x(mine).astype(f32)


def pick(options):
    out = options[-1][1]
    for cond, value in options[-2::-1]:
        out = jnp.where(cond, value, out)
    return out


class Wave:
    def __init__(self, count, n, at):
        self.count, self.n, self.at = count, n, at
        self.right, self.left, self.chunks = [], [], []
        self.steps = count + LAG * max(n - 2, 0) if n > 1 else 0

    def advance(self, chunks):
        n, at = self.n, self.at
        self.chunks = chunks
        while len(self.right) < self.steps:
            s = len(self.right)
            if min(s, self.count - 1) >= len(chunks):
                break
            own_right = [(at == i, chunks[s - LAG * i]) for i in range(n - 1) if 0 <= s - LAG * i < self.count]
            own_left = [(at == n - 1 - i, chunks[s - LAG * i]) for i in range(n - 1) if 0 <= s - LAG * i < self.count]
            go_right, go_left = pick(own_right), pick(own_left)
            if s >= LAG:
                go_right = (go_right.astype(f32) + self.right[s - LAG].astype(f32)).astype(bf16)
                go_left = (go_left.astype(f32) + self.left[s - LAG].astype(f32)).astype(bf16)
            self.right.append(lax.ppermute(go_right, "fsdp", [(i, i + 1) for i in range(n - 1)]))
            self.left.append(lax.ppermute(go_left, "fsdp", [(i + 1, i) for i in range(n - 1)]))

    def total(self, c):
        n, at = self.n, self.at
        own = self.chunks[c].astype(f32)
        if n == 1:
            return own.astype(bf16)
        zero = jnp.zeros((), bf16)
        from_left = pick([(at == j, self.right[c + LAG * (j - 1)]) for j in range(1, n)] + [(None, zero)])
        from_right = pick([(at == j, self.left[c + LAG * (n - 2 - j)]) for j in range(n - 1)] + [(None, zero)])
        return (own + (from_left.astype(f32) + from_right.astype(f32))).astype(bf16)


def spread_kernel(where_ref, mine_ref, core_ref, tile_ref, out_ref):
    t = pl.program_id(0)
    out_ref[...] = jnp.where(mine_ref[t] == 1, tile_ref[...], 0.0).astype(bf16)


def spread_tiles(tile_master, place, mine, core, first, count, half):
    width = tile_master.shape[2]
    return pl.pallas_call(
        spread_kernel,
        grid_spec=pltpu.PrefetchScalarGridSpec(
            num_scalar_prefetch=3,
            grid=(count,),
            in_specs=[pl.BlockSpec((1, half, width), lambda t, w, m, c: (w[t], c[0], 0))],
            out_specs=pl.BlockSpec((1, half, width), lambda t, w, m, c: (t, 0, 0)),
        ),
        out_shape=jax.ShapeDtypeStruct((count, half, width), bf16),
        name="spread_tiles",
    )(place[first:first + count], mine[first:first + count], core, tile_master)


def adamw_update(weight, moment_one, moment_two, gradient, rate):
    moment_one = beta_first * moment_one + (1.0 - beta_first) * gradient
    moment_two = beta_second * moment_two + (1.0 - beta_second) * gradient * gradient
    first_hat = moment_one / (1.0 - beta_first**STEP)
    second_hat = moment_two / (1.0 - beta_second**STEP)
    weight = weight - rate * (first_hat / (jnp.sqrt(second_hat) + adam_eps) + weight_decay * weight)
    return (weight, moment_one, moment_two)


def tile_adamw_kernel(tile_ref, used_ref, core_ref, w_ref, m_ref, v_ref, g_ref, w_out, m_out, v_out):
    slot = pl.program_id(0)

    @pl.when(used_ref[slot] == 1)
    def _():
        new = adamw_update(w_ref[...], m_ref[...], v_ref[...], g_ref[0].astype(f32), learn_rate)
        w_out[...], m_out[...], v_out[...] = new

    @pl.when(used_ref[slot] != 1)
    def _():
        w_out[...], m_out[...], v_out[...] = w_ref[...], m_ref[...], v_ref[...]


def tile_adamw(tile_of, used, core, weight, first, second, grads):
    slots, rows, width = weight.shape
    half = rows // 2
    block = pl.BlockSpec((1, half, width), lambda s, h, t, u, c: (s, h, 0))
    grad_block = pl.BlockSpec((1, 1, half, width), lambda s, h, t, u, c: (h ^ c[0], t[s], 0, 0))
    return pl.pallas_call(
        tile_adamw_kernel,
        grid_spec=pltpu.PrefetchScalarGridSpec(
            num_scalar_prefetch=3,
            grid=(slots, 2),
            in_specs=[block, block, block, grad_block],
            out_specs=[block, block, block],
        ),
        out_shape=[jax.ShapeDtypeStruct(weight.shape, f32)] * 3,
        name="tile_adamw",
    )(tile_of, used, core, weight, first, second, grads)


def line_parts(take, n, at):
    got = []
    for m in range(-(n - 1), n):
        k = -m
        part = take(jnp.clip(at + k, 0, n - 1))
        if m:
            part = lax.ppermute(part, "fsdp", [(i, i + k) for i in range(n) if 0 <= i + k < n])
        got.append(part)
    return lax.dynamic_slice_in_dim(jnp.stack(got), n - 1 - at, n, 0)


def sum_all(v, axes, n):
    for axis in axes:
        if axis == "fsdp":
            bit = 1
            while bit < n:
                v = v + lax.ppermute(v, "fsdp", [(i, i ^ bit) for i in range(n)])
                bit *= 2
        elif axis == "ctx":
            v = v + over_core(v)
        elif axis == "x":
            v = v + over_x(v)
        else:
            v = v + over_y(v)
    return v


def turn(v, bit, axis):
    half = v.shape[axis] // 2
    a = lax.slice_in_dim(v, 0, half, axis=axis)
    b = lax.slice_in_dim(v, half, 2 * half, axis=axis)
    return lax.concatenate([jnp.where(bit == 1, b, a), jnp.where(bit == 1, a, b)], axis)


def by_place(v, index, bits, axis):
    size = v.shape[axis] >> bits
    shape = v.shape[:axis] + (2,) * bits + (size,) + v.shape[axis + 1:]
    v = v.reshape(shape)
    for b in range(bits):
        v = turn(v, (index >> (bits - 1 - b)) & 1, axis + b)
    return v.reshape(v.shape[:axis] + (size << bits,) + v.shape[axis + bits + 1:])


def swap_rows(kv, outer, piece):
    v = kv.reshape(2, 2, 2, piece, kv.shape[-1])
    v = v[:, ::-1] if outer else v[:, :, ::-1]
    return v.reshape(kv.shape)


def body(
    token_ids,
    masked,
    tile_slot,
    tile_master,
    tile_first,
    tile_second,
    embedding,
    embed_first,
    embed_second,
    position_table,
    position_first,
    position_second,
    norm_params,
    norm_first,
    norm_second,
    head_bias,
    bias_first,
    bias_second,
):
    n = lax.axis_size("fsdp")
    z = lax.axis_index("fsdp")
    core = lax.axis_index("ctx")
    tp = lax.axis_index("tp")
    tx, ty = tp % 2, tp // 2
    slots, width, model = tile_master.shape
    half = width // 2
    columns = 2 * width
    heads = columns // HEAD_DIM
    half_len = token_ids.shape[1]
    rows = half_len // 2
    share = rows // 2
    own_dim = embedding.shape[0]
    norms = norm_params.shape[1]
    core_arr = core.reshape(1).astype(jnp.int32)

    ids_half = jnp.where(masked == 1, VOCAB - 1, token_ids)
    ids = lax.dynamic_slice(ids_half, (0, ty * rows), (1, rows))
    count = sum_all(
        jnp.broadcast_to(jnp.sum(masked).astype(f32), (8, 128)), ("fsdp", "ctx"), n
    )[0, 0]

    local = tile_slot - z * slots
    mine = ((local >= 0) & (local < slots)).astype(jnp.int32)
    place = jnp.clip(local, 0, slots - 1)
    own_tiles = spread_tiles(tile_master, place, mine, core_arr, 0, TILES, half)
    chunk_count = TILES // GROUP
    wave = Wave(chunk_count, n, z)
    wave.advance([own_tiles[c * GROUP:(c + 1) * GROUP] for c in range(chunk_count)])

    def full_rows(c):
        own = wave.total(c)
        both = jnp.stack([own, over_y(own)], 1)
        every = jnp.stack([both, over_core(both)], 1)
        return every.reshape(GROUP, columns, model)

    block_at = core * 4 + tp
    vocab_pad = 8 * BLOCK - VOCAB
    embed_pad = jnp.pad(embedding.astype(bf16), ((0, 0), (0, vocab_pad)))
    packed = jnp.concatenate(
        [
            lax.dynamic_slice(embed_pad, (0, block_at * BLOCK), (own_dim, BLOCK)),
            lax.dynamic_slice(
                position_table, (0, core * half_len + ty * rows), (own_dim, rows)
            ).astype(bf16),
            jnp.pad(
                norm_params.astype(bf16).reshape(2 * norms, own_dim).T, ((0, 0), (0, 128 - 2 * norms))
            ),
        ],
        1,
    )
    tables = line_parts(lambda j: packed, n, z).reshape(model, BLOCK + rows + 128)
    embed_own = tables[:, :BLOCK]
    places_own = tables[:, BLOCK:BLOCK + rows].T.astype(f32)
    gains = tables[:, BLOCK + rows:BLOCK + rows + 2 * norms].T.reshape(2, norms, model).astype(f32)
    embed_two = jnp.concatenate([embed_own, over_x(embed_own)], 1)
    embed_four = jnp.concatenate([embed_two, over_y(embed_two)], 1)
    embed_all = jnp.concatenate([embed_four, over_core(embed_four)], 1)

    def own_column(token):
        return (((token // BLOCK) ^ block_at) * BLOCK) + token % BLOCK

    column_at = lax.broadcasted_iota(jnp.int32, (1, 8 * BLOCK), 1)
    real = own_column(column_at) < VOCAB
    pick_ids = (own_column(ids).reshape(rows, 1) == column_at).astype(bf16)
    stream = dot(pick_ids, embed_all, ((1,), (1,))) + places_own

    all_ids = line_parts(lambda j: ids, n, z).reshape(n, 1, rows)
    all_ids = jnp.concatenate([all_ids, over_y(all_ids)], 1)
    all_ids = jnp.concatenate([all_ids, over_core(all_ids)], 1)

    scale = HEAD_DIM ** (-0.5)
    weights, kept_layers = [], []
    for layer in range(LAYERS):
        first = layer * 12 // GROUP
        got = [full_rows(c) for c in range(first, first + 12 // GROUP)]
        tiles = jnp.concatenate(got, 0)
        w_qkv = tiles[0:3].reshape(3 * columns, model)
        w_o = tiles[3]
        w_in = tiles[4:8].reshape(4 * columns, model)
        w_out = tiles[8:12].reshape(4 * columns, model)
        weights.append((w_qkv, w_o, w_in, w_out))
        normed = norm_parts(stream, gains[0, 2 * layer], gains[1, 2 * layer])[0].astype(bf16)
        kv = dot(w_qkv[columns:], normed, ((1,), (1,))).astype(bf16)
        kv_two = jnp.stack([kv, swap_rows(over_y(kv), False, half)])
        kv_other = over_core(kv_two)
        kv_other = jnp.stack([swap_rows(kv_other[0], True, half), swap_rows(kv_other[1], True, half)])
        kv_all = jnp.concatenate([kv_two, kv_other], 0)
        kv_all = kv_all.transpose(1, 0, 2).reshape(2, heads, HEAD_DIM, 4 * rows)
        queries = dot(w_qkv[:columns], normed, ((1,), (1,))).astype(bf16).reshape(heads, HEAD_DIM, rows)
        keys, values = kv_all[0], kv_all[1]
        scores = jnp.einsum("hcq,hck->hqk", queries, keys, preferred_element_type=f32) * scale
        row_top = jnp.max(scores, -1, keepdims=True)
        log_total = row_top + jnp.log(jnp.sum(jnp.exp(scores - row_top), -1, keepdims=True))
        attn = jnp.exp(scores - log_total).astype(bf16)
        mixed = (
            jnp.einsum("hqk,hck->hcq", attn, values, preferred_element_type=f32)
            .astype(bf16)
            .reshape(columns, rows)
        )
        middle = stream + sum_over_x(dot(mixed, w_o, ((0,), (0,))))
        normed_mlp = norm_parts(middle, gains[0, 2 * layer + 1], gains[1, 2 * layer + 1])[0].astype(bf16)
        pre_gelu = dot(normed_mlp, w_in, ((1,), (1,)))
        activation = jax.nn.gelu(pre_gelu, approximate=False).astype(bf16)
        kept_layers.append((stream, middle, queries, keys, values, log_total, mixed, pre_gelu))
        stream = middle + sum_over_x(dot(activation, w_out, ((1,), (0,))))

    final_rows = lax.dynamic_slice_in_dim(stream, tx * share, share, 0)
    final_normed, hat_final, inv_final = norm_parts(final_rows, gains[0, 2 * LAYERS], gains[1, 2 * LAYERS])
    final_normed = final_normed.astype(bf16)
    bias_own = by_place(jnp.pad(head_bias, (0, vocab_pad)).reshape(1, 8 * BLOCK), block_at, 3, 1)
    logits = dot(final_normed, embed_all, ((1,), (0,))) + bias_own
    logits = jnp.where(real, logits, -1e30)
    start = ty * rows + tx * share
    targets = lax.dynamic_slice(token_ids, (0, start), (1, share)).reshape(share, 1)
    row_weights = lax.dynamic_slice(masked, (0, start), (1, share)).reshape(share, 1).astype(f32)
    row_top = jnp.max(logits, -1, keepdims=True)
    log_total = row_top + jnp.log(jnp.sum(jnp.exp(logits - row_top), -1, keepdims=True))
    is_target = own_column(targets) == column_at
    picked = jnp.sum(jnp.where(is_target, logits, 0.0), -1, keepdims=True)
    loss_part = jnp.sum((log_total - picked) * row_weights)
    grad_logits = (
        (jnp.exp(logits - log_total) - is_target.astype(f32)) * (row_weights / count)
    ).astype(bf16)
    bias_part = by_place(jnp.sum(grad_logits.astype(f32), 0, keepdims=True), block_at, 3, 1)
    bias_part = jnp.where(column_at == 8 * BLOCK - 1, loss_part, bias_part)
    bias_sum = sum_all(bias_part, ("x", "y", "ctx", "fsdp"), n)
    bias_grad = bias_sum[0, :VOCAB]
    loss_value = bias_sum[0, 8 * BLOCK - 1] / count
    grad_final = dot(grad_logits, embed_all, ((1,), (1,)))
    part = norm_back(grad_final, hat_final, inv_final, gains[0, 2 * LAYERS]).astype(bf16)
    other = over_x(part)
    gradient = jnp.concatenate(
        [jnp.where(tx == 0, part, other), jnp.where(tx == 0, other, part)], 0
    ).astype(f32)
    final_norm_grad = jnp.stack([jnp.sum(grad_final * hat_final, 0), jnp.sum(grad_final, 0)])
    final_norm_grad = final_norm_grad + over_x(final_norm_grad)

    embed_part = dot(final_normed, grad_logits, ((0,), (0,))).astype(bf16)

    def fold(v, send):
        cut = v.shape[1] // 2
        return (v[:, :cut].astype(f32) + send(v[:, cut:]).astype(f32)).astype(bf16)

    embed_part = fold(fold(fold(embed_part, over_core), over_y), over_x)
    embed_head = line_parts(
        lambda j: lax.dynamic_slice_in_dim(embed_part, j * own_dim, own_dim, 0), n, z
    )
    embed_head = jnp.sum(embed_head.astype(f32), 0).astype(bf16)
    embed_head = jnp.concatenate([embed_head, over_x(embed_head)], 1)
    embed_head = jnp.concatenate([embed_head, over_y(embed_head)], 1)
    embed_head = jnp.concatenate([embed_head, over_core(embed_head)], 1)

    norm_grads = [None] * norms
    norm_grads[2 * LAYERS] = final_norm_grad
    back = Wave(chunk_count, n, z)
    order, chunks = [], []

    def reduce_tiles(grads, first):
        for c in range(grads.shape[0] // GROUP):
            g = grads[c * GROUP:(c + 1) * GROUP].astype(bf16)
            g = fold(g, over_core)
            g = fold(g, over_y)
            order.append(first // GROUP + c)
            chunks.append(g)
        back.advance(chunks)

    for layer in reversed(range(LAYERS)):
        stream, middle, queries, keys, values, log_total, mixed, pre_gelu = kept_layers[layer]
        w_qkv, w_o, w_in, w_out = weights[layer]
        branch = gradient.astype(bf16)
        activation = jax.nn.gelu(pre_gelu, approximate=False).astype(bf16)
        grad_out = dot(activation, branch, ((0,), (0,))).reshape(4, columns, model)
        reduce_tiles(grad_out, 12 * layer + 8)
        grad_act = dot(branch, w_out, ((1,), (1,)))
        grad_pre = (grad_act * gelu_slope(pre_gelu)).astype(bf16)
        normed_mlp, hat_mlp, inv_mlp = norm_parts(middle, gains[0, 2 * layer + 1], gains[1, 2 * layer + 1])
        grad_normed = sum_over_x(dot(grad_pre, w_in, ((1,), (0,))))
        grad_in = dot(grad_pre, normed_mlp.astype(bf16), ((0,), (0,))).reshape(4, columns, model)
        reduce_tiles(grad_in, 12 * layer + 4)
        grad_middle = gradient + norm_back(grad_normed, hat_mlp, inv_mlp, gains[0, 2 * layer + 1])
        norm_grads[2 * layer + 1] = jnp.stack([jnp.sum(grad_normed * hat_mlp, 0), jnp.sum(grad_normed, 0)])
        branch = grad_middle.astype(bf16)
        grad_proj_out = dot(mixed, branch, ((1,), (0,)))
        grad_mixed = dot(w_o, branch, ((1,), (1,))).astype(bf16).reshape(heads, HEAD_DIM, rows)
        soft = jnp.exp(
            jnp.einsum("hcq,hck->hqk", queries, keys, preferred_element_type=f32) * scale - log_total
        )
        grad_soft = jnp.einsum("hcq,hck->hqk", grad_mixed, values, preferred_element_type=f32)
        grad_scores = (soft * (grad_soft - jnp.sum(soft * grad_soft, -1, keepdims=True))).astype(bf16)
        grad_keys = jnp.einsum("hcq,hqk->hck", queries, grad_scores, preferred_element_type=f32) * scale
        grad_values = jnp.einsum("hcq,hqk->hck", grad_mixed, soft.astype(bf16), preferred_element_type=f32)
        grad_queries = jnp.einsum("hck,hqk->hcq", keys, grad_scores, preferred_element_type=f32) * scale
        grad_kv = jnp.stack([grad_keys, grad_values]).astype(bf16).reshape(2 * columns, 4, rows)
        grad_kv = grad_kv.transpose(1, 0, 2)
        from_core = over_core(grad_kv[2:4])
        pair = [
            grad_kv[i].astype(f32) + swap_rows(from_core[i], True, half).astype(f32) for i in range(2)
        ]
        from_y = swap_rows(over_y(pair[1].astype(bf16)), False, half)
        grad_kv = (pair[0] + from_y.astype(f32)).astype(bf16)
        grad_qkv = jnp.concatenate([grad_queries.astype(bf16).reshape(columns, rows), grad_kv], 0)
        normed, hat_attn, inv_attn = norm_parts(stream, gains[0, 2 * layer], gains[1, 2 * layer])
        grad_normed = sum_over_x(dot(grad_qkv, w_qkv, ((0,), (0,))))
        grad_w = dot(grad_qkv, normed.astype(bf16), ((1,), (0,)))
        grad_w = jnp.concatenate([grad_w, grad_proj_out], 0).reshape(4, columns, model)
        reduce_tiles(grad_w, 12 * layer)
        gradient = grad_middle + norm_back(grad_normed, hat_attn, inv_attn, gains[0, 2 * layer])
        norm_grads[2 * layer] = jnp.stack([jnp.sum(grad_normed * hat_attn, 0), jnp.sum(grad_normed, 0)])

    norm_rows = jnp.stack(norm_grads, 1).reshape(2 * norms, model)
    state = jnp.concatenate(
        [gradient.astype(bf16), norm_rows.astype(bf16), jnp.zeros((16 - 2 * norms, model), bf16)], 0
    )
    state = state.reshape(rows + 16, n, own_dim).transpose(1, 0, 2)
    state = line_parts(lambda j: lax.dynamic_index_in_dim(state, j, 0, False), n, z)[:, None]
    state = jnp.concatenate([state, over_y(state)], 1)
    state = jnp.concatenate([state, over_core(state)], 1)
    norm_grad = jnp.sum(state[:, :, rows:rows + 2 * norms].astype(f32), (0, 1)).reshape(2, norms, own_dim)
    token_grads = state[:, :, :rows]
    position_grad = jnp.sum(token_grads.astype(f32), 0).reshape(4 * rows, own_dim)
    position_grad = by_place(position_grad, core * 2 + ty, 2, 0).T
    choose = (all_ids.reshape(n * 4 * rows, 1) == column_at).astype(bf16)
    embed_tail = dot(token_grads.reshape(n * 4 * rows, own_dim), choose, ((0,), (0,)))
    embed_grad = (embed_tail + by_place(embed_head, block_at, 3, 1).astype(f32))[:, :VOCAB]

    halves = [None] * chunk_count
    for i, c in enumerate(order):
        own = back.total(i)
        halves[c] = jnp.stack([own, over_core(own)])
    grads = jnp.concatenate(halves, 1)
    is_slot = (z * slots + jnp.arange(slots, dtype=jnp.int32))[:, None] == tile_slot[None, :]
    used = jnp.any(is_slot, 1).astype(jnp.int32)
    tile_of = jnp.sum(jnp.where(is_slot, jnp.arange(TILES, dtype=jnp.int32)[None, :], 0), 1)
    tile_upd = tile_adamw(tile_of, used, core_arr, tile_master, tile_first, tile_second, grads)
    embed_upd = adamw_update(embedding, embed_first, embed_second, embed_grad, learn_rate)
    position_upd = adamw_update(position_table, position_first, position_second, position_grad, learn_rate)
    norm_upd = adamw_update(norm_params, norm_first, norm_second, norm_grad, small_rate)
    bias_upd = adamw_update(head_bias, bias_first, bias_second, bias_grad, small_rate)
    return (loss_value, *tile_upd, *embed_upd, *position_upd, *norm_upd, *bias_upd)


def solution(mesh):
    halves, tiles, table = P("fsdp", "ctx"), P("fsdp", "tp", None), P("fsdp", None)
    norms, copied = P(None, None, "fsdp"), P()
    three = lambda spec: (spec,) * 3
    return jax.shard_map(
        body,
        mesh=mesh,
        in_specs=(halves, halves, copied, *three(tiles), *three(table), *three(table), *three(norms), *three(copied)),
        out_specs=(copied, *three(tiles), *three(table), *three(table), *three(norms), *three(copied)),
        check_vma=False,
    )
```

```python
import jax
import jax.numpy as jnp
from jax import lax
from jax.experimental import pallas as pl
from jax.experimental.pallas import tpu as pltpu
from jax.sharding import Mesh
from jax.sharding import PartitionSpec as P

HEAD_DIM = 48
VOCAB = 2025
LAYERS = 3
STEP = 10
TILES = 36
BLOCK = 256

norm_eps = 1e-05
beta_first = 0.9
beta_second = 0.999
learn_rate = 0.05
small_rate = 0.5
weight_decay = 0.01
adam_eps = 1e-08

bf16 = jnp.bfloat16
f32 = jnp.float32
FLIP = [(0, 1), (1, 0)]
PLANE = ("ctx", "ty", "tx")
EVERY = ("fsdp", "ctx", "ty", "tx")


def over(axis, v):
    return lax.ppermute(v, axis, FLIP)


def dot(left, right, dims):
    return lax.dot_general(left, right, (dims, ((), ())), preferred_element_type=f32)


def norm_parts(stream, gain, shift):
    centered = stream - jnp.mean(stream, -1, keepdims=True)
    inverse = lax.rsqrt(jnp.mean(centered * centered, -1, keepdims=True) + norm_eps)
    normal_hat = centered * inverse
    return (normal_hat * gain + shift, normal_hat, inverse)


def norm_back(gradient, normal_hat, inverse, gain):
    scaled = gradient * gain
    return inverse * (
        scaled
        - jnp.mean(scaled, -1, keepdims=True)
        - normal_hat * jnp.mean(scaled * normal_hat, -1, keepdims=True)
    )


def gelu_slope(pre_gelu):
    return (
        0.5 * (1.0 + lax.erf(pre_gelu * 0.7071067811865476))
        + pre_gelu * jnp.exp(-0.5 * pre_gelu * pre_gelu) * 0.3989422804014327
    )


def sum_over_x(partial):
    mine = partial.astype(bf16)
    return mine.astype(f32) + over("tx", mine).astype(f32)


def add_halves(keep, come):
    return (keep.astype(f32) + come.astype(f32)).astype(bf16)


def choose(bit, one, zero):
    return jnp.where(bit == 1, one, zero)


def both(axis, v, at, dim):
    other = over(axis, v)
    return lax.concatenate([choose(at, other, v), choose(at, v, other)], dim)


def after(value, event):
    return lax.optimization_barrier((value, event))[0]


def order_kernel(slot_ref, held_ref, out_ref):
    out_ref[0] = held_ref[0, :, 0]


def order_tiles(held, slot, first, count):
    _, pieces, slots, half, model = held.shape
    return pl.pallas_call(
        order_kernel,
        grid_spec=pltpu.PrefetchScalarGridSpec(
            num_scalar_prefetch=1,
            grid=(count,),
            in_specs=[
                pl.BlockSpec((1, pieces, 1, half, model), lambda t, s: (s[t] // slots, 0, s[t] % slots, 0, 0))
            ],
            out_specs=pl.BlockSpec((1, pieces, half, model), lambda t, s: (t, 0, 0, 0)),
        ),
        out_shape=jax.ShapeDtypeStruct((count, pieces, half, model), bf16),
        name="order_tiles",
    )(slot[first:first + count], held)


def adamw_update(weight, moment_one, moment_two, gradient, rate):
    moment_one = beta_first * moment_one + (1.0 - beta_first) * gradient
    moment_two = beta_second * moment_two + (1.0 - beta_second) * gradient * gradient
    first_hat = moment_one / (1.0 - beta_first**STEP)
    second_hat = moment_two / (1.0 - beta_second**STEP)
    weight = weight - rate * (first_hat / (jnp.sqrt(second_hat) + adam_eps) + weight_decay * weight)
    return (weight, moment_one, moment_two)


def tile_adamw_kernel(tile_ref, used_ref, core_ref, w_ref, m_ref, v_ref, low_ref, high_ref, w_out, m_out, v_out):
    slot = pl.program_id(0)
    half = low_ref.shape[2]

    @pl.when(used_ref[slot] == 1)
    def _():
        for h, g_ref in enumerate((low_ref, high_ref)):
            at = pl.ds(h * half, half)
            new = adamw_update(w_ref[0, at], m_ref[0, at], v_ref[0, at], g_ref[0, 0].astype(f32), learn_rate)
            w_out[0, at], m_out[0, at], v_out[0, at] = new

    @pl.when(used_ref[slot] != 1)
    def _():
        w_out[...], m_out[...], v_out[...] = w_ref[...], m_ref[...], v_ref[...]


def tile_adamw(tile_of, used, core, weight, first, second, grads):
    slots, rows, width = weight.shape
    half = rows // 2
    block = pl.BlockSpec((1, rows, width), lambda s, t, u, c: (s, 0, 0))
    low = pl.BlockSpec((1, 1, half, width), lambda s, t, u, c: (c[0], t[s], 0, 0))
    high = pl.BlockSpec((1, 1, half, width), lambda s, t, u, c: (1 - c[0], t[s], 0, 0))
    return pl.pallas_call(
        tile_adamw_kernel,
        grid_spec=pltpu.PrefetchScalarGridSpec(
            num_scalar_prefetch=3,
            grid=(slots,),
            in_specs=[block, block, block, low, high],
            out_specs=[block, block, block],
        ),
        out_shape=[jax.ShapeDtypeStruct(weight.shape, f32)] * 3,
        compiler_params=pltpu.CompilerParams(vmem_limit_bytes=32 * 2**20),
        name="tile_adamw",
    )(tile_of, used, core, weight, first, second, grads, grads)


def body(
    token_ids,
    masked,
    tile_slot,
    tile_master,
    tile_first,
    tile_second,
    embedding,
    embed_first,
    embed_second,
    position_table,
    position_first,
    position_second,
    norm_params,
    norm_first,
    norm_second,
    head_bias,
    bias_first,
    bias_second,
):
    n = lax.axis_size("fsdp")
    z, core, ty, tx = (lax.axis_index(a) for a in EVERY)
    slots, width, model = tile_master.shape
    half = width // 2
    columns = 2 * width
    heads = columns // HEAD_DIM
    half_len = token_ids.shape[1]
    rows = half_len // 2
    share = rows // 2
    own_dim = embedding.shape[0]
    norms = norm_params.shape[1]
    core_arr = core.reshape(1).astype(jnp.int32)
    piece_at = core * 2 + ty

    held = lax.dynamic_slice(tile_master, (0, core * half, 0), (slots, half, model)).astype(bf16)

    held = lax.all_gather(held, ("fsdp", "ctx", "ty"), axis=0, tiled=True).reshape(n, 4, slots, half, model)

    block_at = piece_at * 2 + tx
    vocab_pad = 8 * BLOCK - VOCAB
    wide = BLOCK + rows
    embed_pad = jnp.pad(embedding.astype(bf16), ((0, 0), (0, vocab_pad)))
    ids_half = jnp.where(masked == 1, VOCAB - 1, token_ids)
    ids = lax.dynamic_slice(ids_half, (0, ty * rows), (1, rows))
    coded = lax.dynamic_slice(ids_half * 2 + masked, (0, ty * rows), (1, rows))
    coded = jnp.concatenate([coded // 256, coded % 256], 1).astype(bf16)
    packed = jnp.concatenate(
        [
            lax.dynamic_slice(embed_pad, (0, block_at * BLOCK), (own_dim, BLOCK)),
            lax.dynamic_slice(position_table, (0, piece_at * rows), (own_dim, rows)).astype(bf16),
        ],
        1,
    )
    packed = jnp.concatenate(
        [
            packed,
            jnp.pad(norm_params.astype(bf16).reshape(2 * norms, own_dim), ((0, 0), (0, wide - own_dim))),
            jnp.pad(coded, ((0, 15 - 2 * norms), (0, wide - 2 * rows))),
        ],
        0,
    )
    tables = lax.all_gather(packed, "fsdp", axis=0)
    embed_all = tables[:, :own_dim, :BLOCK].reshape(model, BLOCK)
    for axis, at in (("tx", tx), ("ty", ty), ("ctx", core)):
        embed_all = both(axis, embed_all, at, 1)
    places_own = tables[:, :own_dim, BLOCK:].reshape(model, rows).T.astype(f32)
    gains = tables[:, own_dim:own_dim + 2 * norms, :own_dim].transpose(1, 0, 2)
    gains = gains.reshape(2, norms, model).astype(f32)
    coded = tables[:, own_dim + 2 * norms, :2 * rows].reshape(n, 1, 2, rows)
    for axis, at in (("ty", ty), ("ctx", core)):
        coded = both(axis, coded, at, 1)
    coded = coded.astype(f32).astype(jnp.int32)
    coded = coded[:, :, 0] * 256 + coded[:, :, 1]
    all_ids = coded // 2
    count = jnp.sum(coded % 2).astype(f32)
    column_at = lax.broadcasted_iota(jnp.int32, (1, 8 * BLOCK), 1)
    pick_ids = (ids.reshape(rows, 1) == column_at).astype(bf16)
    stream = dot(pick_ids, embed_all, ((1,), (1,))) + places_own

    scale = HEAD_DIM ** (-0.5)
    weights, kept_layers = [], []
    for layer in range(LAYERS):
        tiles = order_tiles(held, tile_slot, 12 * layer, 12)
        tiles = tiles.reshape(12 * columns, model)
        w_qkv, w_o = tiles[:3 * columns], tiles[3 * columns:4 * columns]
        w_in, w_out = tiles[4 * columns:8 * columns], tiles[8 * columns:]
        weights.append((w_qkv, w_o, w_in, w_out))
        normed = norm_parts(stream, gains[0, 2 * layer], gains[1, 2 * layer])[0].astype(bf16)
        kv = dot(w_qkv[columns:], normed, ((1,), (1,))).astype(bf16)
        kv_two = jnp.concatenate([kv, over("ty", kv)], 1)
        kv_all = jnp.concatenate([kv_two, over("ctx", kv_two)], 1).reshape(2, heads, HEAD_DIM, 4 * rows)
        queries = dot(w_qkv[:columns], normed, ((1,), (1,))).astype(bf16).reshape(heads, HEAD_DIM, rows)
        keys, values = kv_all[0], kv_all[1]
        scores = jnp.einsum("hcq,hck->hqk", queries, keys, preferred_element_type=f32) * scale
        row_top = jnp.max(scores, -1, keepdims=True)
        log_total = row_top + jnp.log(jnp.sum(jnp.exp(scores - row_top), -1, keepdims=True))
        attn = jnp.exp(scores - log_total).astype(bf16)
        mixed = (
            jnp.einsum("hqk,hck->hcq", attn, values, preferred_element_type=f32)
            .astype(bf16)
            .reshape(columns, rows)
        )
        middle = stream + sum_over_x(dot(mixed, w_o, ((0,), (0,))))
        normed_mlp = norm_parts(middle, gains[0, 2 * layer + 1], gains[1, 2 * layer + 1])[0].astype(bf16)
        pre_gelu = dot(normed_mlp, w_in, ((1,), (1,)))
        activation = jax.nn.gelu(pre_gelu, approximate=False).astype(bf16)
        kept_layers.append((stream, middle, queries, keys, values, log_total, mixed, pre_gelu))
        stream = middle + sum_over_x(dot(activation, w_out, ((1,), (0,))))

    final_rows = lax.dynamic_slice_in_dim(stream, tx * share, share, 0)
    final_normed, hat_final, inv_final = norm_parts(final_rows, gains[0, 2 * LAYERS], gains[1, 2 * LAYERS])
    final_normed = final_normed.astype(bf16)
    bias_row = jnp.pad(head_bias, (0, vocab_pad)).reshape(1, 8 * BLOCK)
    logits = dot(final_normed, embed_all, ((1,), (0,))) + bias_row
    logits = jnp.where(column_at < VOCAB, logits, -1e30)
    start = ty * rows + tx * share
    targets = lax.dynamic_slice(token_ids, (0, start), (1, share)).reshape(share, 1)
    row_weights = lax.dynamic_slice(masked, (0, start), (1, share)).reshape(share, 1).astype(f32)
    row_top = jnp.max(logits, -1, keepdims=True)
    log_total = row_top + jnp.log(jnp.sum(jnp.exp(logits - row_top), -1, keepdims=True))
    is_target = targets == column_at
    picked = jnp.sum(jnp.where(is_target, logits, 0.0), -1, keepdims=True)
    loss_part = jnp.sum((log_total - picked) * row_weights)
    grad_logits = (
        (jnp.exp(logits - log_total) - is_target.astype(f32)) * (row_weights / count)
    ).astype(bf16)
    bias_sum = jnp.sum(grad_logits.astype(f32), 0, keepdims=True)
    bias_sum = jnp.where(column_at == 8 * BLOCK - 1, loss_part, bias_sum)
    for axis in PLANE:
        bias_sum = bias_sum + over(axis, bias_sum)
    bit = 1
    while bit < n:
        bias_sum = bias_sum + lax.ppermute(bias_sum, "fsdp", [(i, i ^ bit) for i in range(n)])
        bit *= 2
    bias_grad = bias_sum[0, :VOCAB]
    loss_value = bias_sum[0, 8 * BLOCK - 1] / count
    grad_final = dot(grad_logits, embed_all, ((1,), (1,)))
    part = norm_back(grad_final, hat_final, inv_final, gains[0, 2 * LAYERS]).astype(bf16)
    gradient = both("tx", part, tx, 0).astype(f32)
    final_norm_grad = jnp.stack([jnp.sum(grad_final * hat_final, 0), jnp.sum(grad_final, 0)])
    final_norm_grad = final_norm_grad + over("tx", final_norm_grad)

    embed_part = dot(final_normed, grad_logits, ((0,), (0,))).astype(bf16)
    for axis, at in (("ctx", core), ("ty", ty), ("tx", tx)):
        cut = embed_part.shape[1] // 2
        keep = lax.dynamic_slice_in_dim(embed_part, at * cut, cut, 1)
        send = lax.dynamic_slice_in_dim(embed_part, cut - at * cut, cut, 1)
        embed_part = add_halves(keep, over(axis, send))
    embed_head = lax.all_to_all(embed_part.reshape(n, own_dim, BLOCK), "fsdp", 0, 0)
    embed_head = jnp.sum(embed_head.astype(f32), 0).astype(bf16)
    for axis, at in (("tx", tx), ("ty", ty), ("ctx", core)):
        embed_head = both(axis, embed_head, at, 1)

    norm_grads = [None] * norms
    norm_grads[2 * LAYERS] = final_norm_grad
    crossed = []

    def plane_sum(grads):
        keep = lax.dynamic_slice_in_dim(grads, core * 2, 2, 1).astype(bf16)
        send = lax.dynamic_slice_in_dim(grads, 2 - core * 2, 2, 1).astype(bf16)
        two = add_halves(keep, over("ctx", send))
        keep = lax.dynamic_index_in_dim(two, ty, 1, False)
        send = lax.dynamic_index_in_dim(two, 1 - ty, 1, False)
        return add_halves(keep, over("ty", send))

    def cross(own):
        crossed.append(lax.psum(after(own, crossed[-1]) if crossed else own, "fsdp"))

    attn_own = None
    for layer in reversed(range(LAYERS)):
        stream, middle, queries, keys, values, log_total, mixed, pre_gelu = kept_layers[layer]
        w_qkv, w_o, w_in, w_out = weights[layer]
        branch = gradient.astype(bf16)
        activation = jax.nn.gelu(pre_gelu, approximate=False).astype(bf16)
        grad_act = dot(branch, w_out, ((1,), (1,)))
        grad_pre = (grad_act * gelu_slope(pre_gelu)).astype(bf16)
        normed_mlp, hat_mlp, inv_mlp = norm_parts(middle, gains[0, 2 * layer + 1], gains[1, 2 * layer + 1])
        grad_normed = sum_over_x(dot(grad_pre, w_in, ((1,), (0,))))
        grad_out = dot(activation, branch, ((0,), (0,))).reshape(4, 4, half, model)
        grad_in = dot(grad_pre, normed_mlp.astype(bf16), ((0,), (0,))).reshape(4, 4, half, model)
        mlp_own = plane_sum(jnp.concatenate([grad_in, grad_out], 0))
        cross(mlp_own if attn_own is None else jnp.concatenate([mlp_own, attn_own], 0))
        grad_middle = gradient + norm_back(grad_normed, hat_mlp, inv_mlp, gains[0, 2 * layer + 1])
        norm_grads[2 * layer + 1] = jnp.stack([jnp.sum(grad_normed * hat_mlp, 0), jnp.sum(grad_normed, 0)])
        branch = grad_middle.astype(bf16)
        grad_proj_out = dot(mixed, branch, ((1,), (0,)))
        grad_mixed = dot(w_o, branch, ((1,), (1,))).astype(bf16).reshape(heads, HEAD_DIM, rows)
        soft = jnp.exp(
            jnp.einsum("hcq,hck->hqk", queries, keys, preferred_element_type=f32) * scale - log_total
        )
        grad_soft = jnp.einsum("hcq,hck->hqk", grad_mixed, values, preferred_element_type=f32)
        grad_scores = (soft * (grad_soft - jnp.sum(soft * grad_soft, -1, keepdims=True))).astype(bf16)
        grad_keys = jnp.einsum("hcq,hqk->hck", queries, grad_scores, preferred_element_type=f32) * scale
        grad_values = jnp.einsum("hcq,hqk->hck", grad_mixed, soft.astype(bf16), preferred_element_type=f32)
        grad_queries = jnp.einsum("hck,hqk->hcq", keys, grad_scores, preferred_element_type=f32) * scale
        grad_kv = jnp.stack([grad_keys, grad_values]).astype(bf16).reshape(2 * columns, 4 * rows)
        pair = grad_kv[:, :2 * rows].astype(f32) + over("ctx", grad_kv[:, 2 * rows:]).astype(f32)
        grad_kv = (pair[:, :rows] + over("ty", pair[:, rows:].astype(bf16)).astype(f32)).astype(bf16)
        grad_qkv = jnp.concatenate([grad_queries.astype(bf16).reshape(columns, rows), grad_kv], 0)
        normed, hat_attn, inv_attn = norm_parts(stream, gains[0, 2 * layer], gains[1, 2 * layer])
        grad_normed = sum_over_x(dot(grad_qkv, w_qkv, ((0,), (0,))))
        grad_w = dot(grad_qkv, normed.astype(bf16), ((1,), (0,)))
        grad_w = jnp.concatenate([grad_w, grad_proj_out], 0).reshape(4, 4, half, model)
        attn_own = plane_sum(grad_w)
        if layer == 0:
            cross(attn_own)
        gradient = grad_middle + norm_back(grad_normed, hat_attn, inv_attn, gains[0, 2 * layer])
        norm_grads[2 * layer] = jnp.stack([jnp.sum(grad_normed * hat_attn, 0), jnp.sum(grad_normed, 0)])

    norm_rows = jnp.stack(norm_grads, 1).reshape(2 * norms, model)
    state = jnp.concatenate(
        [gradient.astype(bf16), norm_rows.astype(bf16), jnp.zeros((16 - 2 * norms, model), bf16)], 0
    )
    state = state.reshape(rows + 16, n, own_dim).transpose(1, 0, 2)
    state = lax.all_to_all(state, "fsdp", 0, 0)[:, None]
    state = both("ty", state, ty, 1)
    state = both("ctx", state, core, 1)
    norm_grad = jnp.sum(state[:, :, rows:rows + 2 * norms].astype(f32), (0, 1)).reshape(2, norms, own_dim)
    token_grads = state[:, :, :rows]
    position_grad = jnp.sum(token_grads.astype(f32), 0).reshape(4 * rows, own_dim).T
    picks = (all_ids.reshape(n * 4 * rows, 1) == column_at).astype(bf16)
    embed_tail = dot(token_grads.reshape(n * 4 * rows, own_dim), picks, ((0,), (0,)))
    embed_grad = (embed_tail + embed_head.astype(f32))[:, :VOCAB]

    def to_both_cores(own):
        return jnp.stack([own, over("ctx", own)])

    top, middle, bottom, last = (to_both_cores(own) for own in crossed)
    grads = jnp.concatenate(
        [last, bottom[:, :8], bottom[:, 8:], middle[:, :8], middle[:, 8:], top], 1
    )
    is_slot = (z * slots + jnp.arange(slots, dtype=jnp.int32))[:, None] == tile_slot[None, :]
    used = jnp.any(is_slot, 1).astype(jnp.int32)
    tile_of = jnp.sum(jnp.where(is_slot, jnp.arange(TILES, dtype=jnp.int32)[None, :], 0), 1)
    tile_upd = tile_adamw(tile_of, used, core_arr, tile_master, tile_first, tile_second, grads)
    embed_upd = adamw_update(embedding, embed_first, embed_second, embed_grad, learn_rate)
    position_upd = adamw_update(position_table, position_first, position_second, position_grad, learn_rate)
    norm_upd = adamw_update(norm_params, norm_first, norm_second, norm_grad, small_rate)
    bias_upd = adamw_update(head_bias, bias_first, bias_second, bias_grad, small_rate)
    return (loss_value, *tile_upd, *embed_upd, *position_upd, *norm_upd, *bias_upd)


def solution(mesh):
    grid = Mesh(mesh.devices.reshape(-1, 2, 2, 2), EVERY)
    halves, tiles, table = P("fsdp", "ctx"), P("fsdp", ("ty", "tx"), None), P("fsdp", None)
    norms, copied = P(None, None, "fsdp"), P()

    def three(spec):
        return (spec,) * 3

    return jax.shard_map(
        body,
        mesh=grid,
        in_specs=(halves, halves, copied, *three(tiles), *three(table), *three(table), *three(norms), *three(copied)),
        out_specs=(copied, *three(tiles), *three(table), *three(table), *three(norms), *three(copied)),
        check_vma=False,
    )
```

```python
import functools

import jax
import jax.numpy as jnp
from jax import lax
from jax.experimental import pallas as pl
from jax.experimental.pallas import tpu as pltpu
from jax.sharding import Mesh
from jax.sharding import PartitionSpec as P

HEAD_DIM = 48
VOCAB = 2025
LAYERS = 3
STEP = 10
TILES = 36
BLOCK = 256

norm_eps = 1e-05
beta_first = 0.9
beta_second = 0.999
learn_rate = 0.05
small_rate = 0.5
weight_decay = 0.01
adam_eps = 1e-08

bf16 = jnp.bfloat16
f32 = jnp.float32
FLIP = [(0, 1), (1, 0)]
PLANE = ("ctx", "ty", "tx")
EVERY = ("fsdp", "ctx", "ty", "tx")


def over(axis, v):
    return lax.ppermute(v, axis, FLIP)


def dot(left, right, dims):
    return lax.dot_general(left, right, (dims, ((), ())), preferred_element_type=f32)


def norm_parts(stream, gain, shift):
    centered = stream - jnp.mean(stream, -1, keepdims=True)
    inverse = lax.rsqrt(jnp.mean(centered * centered, -1, keepdims=True) + norm_eps)
    normal_hat = centered * inverse
    return (normal_hat * gain + shift, normal_hat, inverse)


def norm_back(gradient, normal_hat, inverse, gain):
    scaled = gradient * gain
    return inverse * (
        scaled
        - jnp.mean(scaled, -1, keepdims=True)
        - normal_hat * jnp.mean(scaled * normal_hat, -1, keepdims=True)
    )


def gelu_slope(pre_gelu):
    return (
        0.5 * (1.0 + lax.erf(pre_gelu * 0.7071067811865476))
        + pre_gelu * jnp.exp(-0.5 * pre_gelu * pre_gelu) * 0.3989422804014327
    )


def sum_over_x(partial):
    mine = partial.astype(bf16)
    return mine.astype(f32) + over("tx", mine).astype(f32)


def add_halves(keep, come):
    return (keep.astype(f32) + come.astype(f32)).astype(bf16)


def choose(bit, one, zero):
    return jnp.where(bit == 1, one, zero)


def both(axis, v, at, dim):
    other = over(axis, v)
    return lax.concatenate([choose(at, other, v), choose(at, v, other)], dim)


def after(value, event):
    return lax.optimization_barrier((value, event))[0]


def needs(value, event):
    first = lax.slice(event, (0,) * event.ndim, (1,) * event.ndim).reshape(())
    return value + jnp.minimum(jnp.abs(first), 0).astype(value.dtype)


def order_kernel(owner_ref, slot_ref, held_ref, out_ref, sem):
    def copy(t):
        return pltpu.make_async_copy(held_ref.at[owner_ref[t], :, slot_ref[t]], out_ref.at[t], sem.at[t])

    for t in range(out_ref.shape[0]):
        copy(t).start()
    for t in range(out_ref.shape[0]):
        copy(t).wait()


def order_tiles(held, owner, slot):
    count, (_, pieces, _, half, model) = owner.shape[0], held.shape
    scalar = pl.BlockSpec(memory_space=pltpu.SMEM)
    return pl.pallas_call(
        order_kernel,
        in_specs=[scalar, scalar, pl.BlockSpec(memory_space=pl.ANY)],
        out_specs=pl.BlockSpec(memory_space=pltpu.VMEM),
        out_shape=jax.ShapeDtypeStruct((count, pieces, half, model), bf16),
        scratch_shapes=[pltpu.SemaphoreType.DMA((count,))],
        compiler_params=pltpu.CompilerParams(vmem_limit_bytes=24 * 2**20),
        name="order_tiles",
    )(owner, slot, held)


def collect_kernel(count, owner_ref, slot_ref, *refs):
    sources, out_ref, sem = refs[:count], refs[-2], refs[-1]

    def copies():
        t = 0
        for source in sources:
            for i in range(source.shape[0]):
                yield pltpu.make_async_copy(source.at[i], out_ref.at[owner_ref[t], slot_ref[t]], sem.at[t])
                t += 1

    for copy in copies():
        copy.start()
    for copy in copies():
        copy.wait()


def collect(sources, owner, slot, n, slots, into=None):
    total, (half, model) = owner.shape[0], sources[0].shape[1:]
    scalar, anywhere = pl.BlockSpec(memory_space=pltpu.SMEM), pl.BlockSpec(memory_space=pl.ANY)
    whole = pl.BlockSpec(memory_space=pltpu.VMEM)
    held = [] if into is None else [into]
    return pl.pallas_call(
        functools.partial(collect_kernel, len(sources)),
        in_specs=[scalar] * 2 + [whole] * len(sources) + [anywhere] * len(held),
        out_specs=anywhere,
        out_shape=jax.ShapeDtypeStruct((n, slots, half, model), bf16),
        input_output_aliases={2 + len(sources): 0} if held else {},
        scratch_shapes=[pltpu.SemaphoreType.DMA((total,))],
        compiler_params=pltpu.CompilerParams(vmem_limit_bytes=24 * 2**20),
        name="collect",
    )(owner, slot, *sources, *held)


def attend_kernel(q_ref, *refs):
    kv_refs, (o_ref, total_ref) = refs[:-2], refs[-2:]
    scale = HEAD_DIM ** (-0.5)
    for i in range(q_ref.shape[0]):
        scores = [dot(kv[0, i], q_ref[i], ((0,), (0,))) * scale for kv in kv_refs]
        top = functools.reduce(jnp.maximum, [jnp.max(s, 0, keepdims=True) for s in scores])
        raised = [jnp.exp(s - top) for s in scores]
        total = sum(jnp.sum(e, 0, keepdims=True) for e in raised)
        share = 1.0 / total
        o_ref[i] = sum(
            dot(kv[1, i], (e * share).astype(bf16), ((1,), (0,))) for kv, e in zip(kv_refs, raised)
        ).astype(bf16)
        total_ref[i] = top + jnp.log(total)


def attend(queries, blocks):
    heads, size, rows = queries.shape
    step = 2
    short = pl.BlockSpec((step, size, rows), lambda h: (h, 0, 0))
    block = pl.BlockSpec((2, step, size, rows), lambda h: (0, h, 0, 0))
    return pl.pallas_call(
        attend_kernel,
        grid=(heads // step,),
        in_specs=[short] + [block] * len(blocks),
        out_specs=[short, pl.BlockSpec((step, 1, rows), lambda h: (h, 0, 0))],
        out_shape=[
            jax.ShapeDtypeStruct((heads, size, rows), bf16),
            jax.ShapeDtypeStruct((heads, 1, rows), f32),
        ],
        compiler_params=pltpu.CompilerParams(vmem_limit_bytes=32 * 2**20),
        name="attend",
    )(queries, *blocks)


def attend_back_kernel(count, q_ref, g_ref, total_ref, *refs):
    kv_refs, dq_ref, dkv_refs = refs[:count], refs[count], refs[count + 1:]
    scale = HEAD_DIM ** (-0.5)
    for i in range(q_ref.shape[0]):
        soft = [jnp.exp(dot(kv[0, i], q_ref[i], ((0,), (0,))) * scale - total_ref[i]) for kv in kv_refs]
        grad_soft = [dot(kv[1, i], g_ref[i], ((0,), (0,))) for kv in kv_refs]
        mean = sum(jnp.sum(p * g, 0, keepdims=True) for p, g in zip(soft, grad_soft))
        grad_scores = [(p * (g - mean)).astype(bf16) for p, g in zip(soft, grad_soft)]
        dq = sum(dot(kv[0, i], ds, ((1,), (0,))) for kv, ds in zip(kv_refs, grad_scores))
        dq_ref[i] = (dq * scale).astype(bf16)
        for dkv, p, ds in zip(dkv_refs, soft, grad_scores):
            dkv[0, i] = (dot(q_ref[i], ds, ((1,), (1,))) * scale).astype(bf16)
            dkv[1, i] = dot(g_ref[i], p.astype(bf16), ((1,), (1,))).astype(bf16)


def attend_back(queries, blocks, gradient, total):
    heads, size, rows = queries.shape
    step = 2
    short = pl.BlockSpec((step, size, rows), lambda h: (h, 0, 0))
    block = pl.BlockSpec((2, step, size, rows), lambda h: (0, h, 0, 0))
    return pl.pallas_call(
        functools.partial(attend_back_kernel, len(blocks)),
        grid=(heads // step,),
        in_specs=[short, short, pl.BlockSpec((step, 1, rows), lambda h: (h, 0, 0))] + [block] * len(blocks),
        out_specs=[short] + [block] * len(blocks),
        out_shape=[jax.ShapeDtypeStruct((heads, size, rows), bf16)]
        + [jax.ShapeDtypeStruct(kv.shape, bf16) for kv in blocks],
        compiler_params=pltpu.CompilerParams(vmem_limit_bytes=32 * 2**20),
        name="attend_back",
    )(queries, gradient, total, *blocks)


def adamw_update(weight, moment_one, moment_two, gradient, rate):
    moment_one = beta_first * moment_one + (1.0 - beta_first) * gradient
    moment_two = beta_second * moment_two + (1.0 - beta_second) * gradient * gradient
    first_hat = moment_one / (1.0 - beta_first**STEP)
    second_hat = moment_two / (1.0 - beta_second**STEP)
    weight = weight - rate * (first_hat / (jnp.sqrt(second_hat) + adam_eps) + weight_decay * weight)
    return (weight, moment_one, moment_two)


def tile_adamw_kernel(used_ref, core_ref, w_ref, m_ref, v_ref, own_ref, oth_ref, w_out, m_out, v_out):
    slot = pl.program_id(0)
    half = w_ref.shape[1] // 2

    @pl.when(used_ref[slot] == 1)
    def _():
        for h, g_ref in enumerate((own_ref, oth_ref)):
            side = core_ref[0] if h == 0 else 1 - core_ref[0]
            at = pl.ds(pl.multiple_of(side * half, half), half)
            new = adamw_update(w_ref[0, at], m_ref[0, at], v_ref[0, at], g_ref[0].astype(f32), learn_rate)
            w_out[0, at], m_out[0, at], v_out[0, at] = new

    @pl.when(used_ref[slot] != 1)
    def _():
        w_out[...], m_out[...], v_out[...] = w_ref[...], m_ref[...], v_ref[...]


def tile_adamw(used, core, state, own, oth):
    slots, rows, width = state[0].shape
    block = pl.BlockSpec((1, rows, width), lambda s, u, c: (s, 0, 0))
    grad_block = pl.BlockSpec((1, rows // 2, width), lambda s, u, c: (s, 0, 0))
    return pl.pallas_call(
        tile_adamw_kernel,
        grid_spec=pltpu.PrefetchScalarGridSpec(
            num_scalar_prefetch=2,
            grid=(slots,),
            in_specs=[block, block, block, grad_block, grad_block],
            out_specs=[block, block, block],
        ),
        out_shape=[jax.ShapeDtypeStruct(state[0].shape, f32)] * 3,
        compiler_params=pltpu.CompilerParams(vmem_limit_bytes=40 * 2**20),
        name="tile_adamw",
    )(used, core, *state, own, oth)


def body(
    token_ids,
    masked,
    tile_slot,
    tile_master,
    tile_first,
    tile_second,
    embedding,
    embed_first,
    embed_second,
    position_table,
    position_first,
    position_second,
    norm_params,
    norm_first,
    norm_second,
    head_bias,
    bias_first,
    bias_second,
):
    n = lax.axis_size("fsdp")
    z, core, ty, tx = (lax.axis_index(a) for a in EVERY)
    slots, width, model = tile_master.shape
    half = width // 2
    columns = 2 * width
    heads = columns // HEAD_DIM
    half_len = token_ids.shape[1]
    rows = half_len // 2
    share = rows // 2
    own_dim = embedding.shape[0]
    norms = norm_params.shape[1]
    core_arr = core.reshape(1).astype(jnp.int32)
    piece_at = core * 2 + ty

    owner = tile_slot // slots
    held = lax.dynamic_slice(tile_master, (0, core * half, 0), (slots, half, model)).astype(bf16)
    held = lax.all_gather(held, ("fsdp", "ctx", "ty"), axis=0, tiled=True).reshape(n, 4, slots, half, model)

    block_at = (core * 2 + tx) * 2 + ty
    vocab_pad = 8 * BLOCK - VOCAB
    wide = BLOCK + rows
    embed_pad = jnp.pad(embedding.astype(bf16), ((0, 0), (0, vocab_pad)))
    ids_half = jnp.where(masked == 1, VOCAB - 1, token_ids)
    ids = lax.dynamic_slice(ids_half, (0, ty * rows), (1, rows))
    coded = lax.dynamic_slice(ids_half * 2 + masked, (0, ty * rows), (1, rows))
    coded = jnp.concatenate([coded // 256, coded % 256], 1).astype(bf16)
    packed = jnp.concatenate(
        [
            lax.dynamic_slice(embed_pad, (0, block_at * BLOCK), (own_dim, BLOCK)),
            lax.dynamic_slice(position_table, (0, piece_at * rows), (own_dim, rows)).astype(bf16),
        ],
        1,
    )
    packed = jnp.concatenate(
        [
            packed,
            jnp.pad(norm_params.astype(bf16).reshape(2 * norms, own_dim), ((0, 0), (0, wide - own_dim))),
            jnp.pad(coded, ((0, 15 - 2 * norms), (0, wide - 2 * rows))),
        ],
        0,
    )
    tables = lax.all_gather(packed, "fsdp", axis=0)
    embed_all = tables[:, :own_dim, :BLOCK].reshape(model, BLOCK)
    for axis, at in (("ty", ty), ("tx", tx), ("ctx", core)):
        embed_all = both(axis, embed_all, at, 1)
    places_own = tables[:, :own_dim, BLOCK:].reshape(model, rows).T.astype(f32)
    gains = tables[:, own_dim:own_dim + 2 * norms, :own_dim].transpose(1, 0, 2)
    gains = gains.reshape(2, norms, model).astype(f32)
    coded = tables[:, own_dim + 2 * norms, :2 * rows].reshape(n, 1, 2, rows)
    for axis, at in (("ty", ty), ("ctx", core)):
        coded = both(axis, coded, at, 1)
    coded = coded.astype(f32).astype(jnp.int32)
    coded = coded[:, :, 0] * 256 + coded[:, :, 1]
    all_ids = coded // 2
    count = jnp.sum(coded % 2).astype(f32)
    column_at = lax.broadcasted_iota(jnp.int32, (1, 8 * BLOCK), 1)
    pick_ids = (ids.reshape(rows, 1) == column_at).astype(bf16)
    stream = dot(pick_ids, embed_all, ((1,), (1,))) + places_own

    weights, kept_layers = [], []
    for layer in range(LAYERS):
        mine = slice(12 * layer, 12 * layer + 12)
        tiles = order_tiles(held, owner[mine], tile_slot[mine] % slots).reshape(12 * columns, model)
        w_qkv, w_o = tiles[:3 * columns], tiles[3 * columns:4 * columns]
        w_in, w_out = tiles[4 * columns:8 * columns], tiles[8 * columns:]
        weights.append((w_qkv, w_o, w_in, w_out))
        normed = norm_parts(stream, gains[0, 2 * layer], gains[1, 2 * layer])[0].astype(bf16)
        kv = dot(w_qkv[columns:], normed, ((1,), (1,))).astype(bf16)
        kv_y = over("ty", kv)
        blocks = [kv, kv_y, over("ctx", kv), over("ctx", kv_y)]
        blocks = [block.reshape(2, heads, HEAD_DIM, rows) for block in blocks]
        queries = dot(w_qkv[:columns], normed, ((1,), (1,))).astype(bf16).reshape(heads, HEAD_DIM, rows)
        mixed, log_total = attend(queries, blocks)
        mixed = mixed.reshape(columns, rows)
        middle = stream + sum_over_x(dot(mixed, w_o, ((0,), (0,))))
        normed_mlp = norm_parts(middle, gains[0, 2 * layer + 1], gains[1, 2 * layer + 1])[0].astype(bf16)
        pre_gelu = dot(normed_mlp, w_in, ((1,), (1,)))
        activation = jax.nn.gelu(pre_gelu, approximate=False).astype(bf16)
        kept_layers.append((stream, middle, queries, blocks, log_total, mixed, pre_gelu))
        stream = middle + sum_over_x(dot(activation, w_out, ((1,), (0,))))

    final_rows = lax.dynamic_slice_in_dim(stream, tx * share, share, 0)
    final_normed, hat_final, inv_final = norm_parts(final_rows, gains[0, 2 * LAYERS], gains[1, 2 * LAYERS])
    final_normed = final_normed.astype(bf16)
    bias_row = jnp.pad(head_bias, (0, vocab_pad)).reshape(1, 8 * BLOCK)
    logits = dot(final_normed, embed_all, ((1,), (0,))) + bias_row
    logits = jnp.where(column_at < VOCAB, logits, -1e30)
    start = ty * rows + tx * share
    targets = lax.dynamic_slice(token_ids, (0, start), (1, share)).reshape(share, 1)
    row_weights = lax.dynamic_slice(masked, (0, start), (1, share)).reshape(share, 1).astype(f32)
    row_top = jnp.max(logits, -1, keepdims=True)
    log_total = row_top + jnp.log(jnp.sum(jnp.exp(logits - row_top), -1, keepdims=True))
    is_target = targets == column_at
    picked = jnp.sum(jnp.where(is_target, logits, 0.0), -1, keepdims=True)
    loss_part = jnp.sum((log_total - picked) * row_weights)
    grad_logits = (
        (jnp.exp(logits - log_total) - is_target.astype(f32)) * (row_weights / count)
    ).astype(bf16)
    bias_sum = jnp.sum(grad_logits.astype(f32), 0, keepdims=True)
    bias_sum = jnp.where(column_at == 8 * BLOCK - 1, loss_part, bias_sum)
    for axis in PLANE:
        bias_sum = bias_sum + over(axis, bias_sum)
    bit = 1
    while bit < n:
        bias_sum = bias_sum + lax.ppermute(bias_sum, "fsdp", [(i, i ^ bit) for i in range(n)])
        bit *= 2
    bias_grad = bias_sum[0, :VOCAB]
    loss_value = bias_sum[0, 8 * BLOCK - 1] / count
    grad_final = dot(grad_logits, embed_all, ((1,), (1,)))
    part = norm_back(grad_final, hat_final, inv_final, gains[0, 2 * LAYERS]).astype(bf16)
    gradient = both("tx", part, tx, 0).astype(f32)
    final_norm_grad = jnp.stack([jnp.sum(grad_final * hat_final, 0), jnp.sum(grad_final, 0)])
    final_norm_grad = final_norm_grad + over("tx", final_norm_grad)

    embed_part = dot(final_normed, grad_logits, ((0,), (0,))).astype(bf16)
    embed_part = lax.psum_scatter(embed_part, "fsdp", scatter_dimension=0, tiled=True)
    offloaded = [embed_part]
    for axis, at in (("ctx", core), ("tx", tx), ("ty", ty)):
        cut = embed_part.shape[1] // 2
        keep = lax.dynamic_slice_in_dim(embed_part, at * cut, cut, 1)
        send = lax.dynamic_slice_in_dim(embed_part, cut - at * cut, cut, 1)
        embed_part = add_halves(keep, over(axis, send))
    embed_head = embed_part
    for axis, at in (("ty", ty), ("tx", tx), ("ctx", core)):
        embed_head = both(axis, embed_head, at, 1)

    norm_grads = [None] * norms
    norm_grads[2 * LAYERS] = final_norm_grad
    tile_grads, tile_list = [], []

    def core_sum(grads):
        keep = lax.dynamic_slice_in_dim(grads, core * 2, 2, 1).astype(bf16)
        send = lax.dynamic_slice_in_dim(grads, 2 - core * 2, 2, 1).astype(bf16)
        return add_halves(keep, over("ctx", send)).transpose(1, 0, 2, 3)

    def neighbour_sum(two):
        keep = lax.dynamic_index_in_dim(two, ty, 0, False)
        send = lax.dynamic_index_in_dim(two, 1 - ty, 0, False)
        return add_halves(keep, over("ty", send))

    def offloaded_sum(flat, axis):
        offloaded.append(lax.psum_scatter(after(flat, offloaded[-1]), axis, scatter_dimension=0, tiled=True))
        return offloaded[-1]

    attn_two = None
    for layer in reversed(range(LAYERS)):
        stream, middle, queries, blocks, log_total, mixed, pre_gelu = kept_layers[layer]
        w_qkv, w_o, w_in, w_out = weights[layer]
        branch = gradient.astype(bf16)
        activation = jax.nn.gelu(pre_gelu, approximate=False).astype(bf16)
        grad_act = dot(branch, w_out, ((1,), (1,)))
        grad_pre = (grad_act * gelu_slope(pre_gelu)).astype(bf16)
        normed_mlp, hat_mlp, inv_mlp = norm_parts(middle, gains[0, 2 * layer + 1], gains[1, 2 * layer + 1])
        partial = dot(grad_pre, w_in, ((1,), (0,))).astype(bf16)
        grad_normed = sum_over_x(partial)
        grad_out = dot(needs(activation, partial), branch, ((0,), (0,))).reshape(4, 4, half, model)
        grad_in = dot(grad_pre, needs(normed_mlp.astype(bf16), partial), ((0,), (0,))).reshape(4, 4, half, model)
        two = core_sum(jnp.concatenate([grad_in, grad_out], 0))
        tile_list += range(12 * layer + 4, 12 * layer + 12)
        if attn_two is not None:
            two = jnp.concatenate([two, attn_two], 1)
            tile_list += range(12 * layer + 12, 12 * layer + 16)
        grad_middle = gradient + norm_back(grad_normed, hat_mlp, inv_mlp, gains[0, 2 * layer + 1])
        norm_grads[2 * layer + 1] = jnp.stack([jnp.sum(grad_normed * hat_mlp, 0), jnp.sum(grad_normed, 0)])
        branch = grad_middle.astype(bf16)
        grad_proj_out = dot(mixed, branch, ((1,), (0,)))
        grad_mixed = dot(w_o, branch, ((1,), (1,))).astype(bf16).reshape(heads, HEAD_DIM, rows)
        grad_queries, kv_own, kv_y, kv_core, kv_both = attend_back(queries, blocks, grad_mixed, log_total)
        kv_own = kv_own.astype(f32) + over("ctx", kv_core).astype(f32)
        from_y = over("ty", add_halves(kv_y, over("ctx", kv_both)))
        grad_kv = (kv_own + from_y.astype(f32)).astype(bf16).reshape(2 * columns, rows)
        two = needs(two, from_y) if layer else two
        tile_grads.append(offloaded_sum(two.reshape(-1, half, model), "ty"))
        grad_qkv = jnp.concatenate([grad_queries.reshape(columns, rows), grad_kv], 0)
        normed, hat_attn, inv_attn = norm_parts(stream, gains[0, 2 * layer], gains[1, 2 * layer])
        partial = dot(grad_qkv, w_qkv, ((0,), (0,))).astype(bf16)
        grad_normed = sum_over_x(partial)
        grad_w = dot(grad_qkv, needs(normed.astype(bf16), partial), ((1,), (0,)))
        grad_w = jnp.concatenate([grad_w, grad_proj_out], 0).reshape(4, 4, half, model)
        attn_two = core_sum(grad_w)
        gradient = grad_middle + norm_back(grad_normed, hat_attn, inv_attn, gains[0, 2 * layer])
        norm_grads[2 * layer] = jnp.stack([jnp.sum(grad_normed * hat_attn, 0), jnp.sum(grad_normed, 0)])

    norm_rows = jnp.stack(norm_grads, 1).reshape(2 * norms, model)
    state = jnp.concatenate(
        [gradient.astype(bf16), norm_rows.astype(bf16), jnp.zeros((16 - 2 * norms, model), bf16)], 0
    )
    state = state.reshape(rows + 16, n, own_dim).transpose(1, 0, 2)
    state = lax.all_to_all(state, "fsdp", 0, 0)[:, None]
    last_grads = needs(neighbour_sum(attn_two), state)
    state = both("ty", state, ty, 1)
    state = both("ctx", state, core, 1)
    norm_grad = jnp.sum(state[:, :, rows:rows + 2 * norms].astype(f32), (0, 1)).reshape(2, norms, own_dim)
    token_grads = state[:, :, :rows]
    position_grad = jnp.sum(token_grads.astype(f32), 0).reshape(4 * rows, own_dim).T
    picks = (all_ids.reshape(n * 4 * rows, 1) == column_at).astype(bf16)
    embed_tail = dot(token_grads.reshape(n * 4 * rows, own_dim), picks, ((0,), (0,)))
    embed_grad = (embed_tail + embed_head.astype(f32))[:, :VOCAB]

    at = jnp.array(tile_list, jnp.int32)
    sent = collect(tile_grads, owner[at], tile_slot[at] % slots, n, slots)
    sent = collect([last_grads], owner[:4], tile_slot[:4] % slots, n, slots, sent)
    tile_sum = offloaded_sum(sent.reshape(-1, half, model), "fsdp")
    used = jnp.any((tile_slot - z * slots)[None, :] == jnp.arange(slots, dtype=jnp.int32)[:, None], 1).astype(jnp.int32)
    state = (tile_master, tile_first, tile_second)
    embed_upd = adamw_update(embedding, embed_first, embed_second, embed_grad, learn_rate)
    position_upd = adamw_update(position_table, position_first, position_second, position_grad, learn_rate)
    norm_upd = adamw_update(norm_params, norm_first, norm_second, norm_grad, small_rate)
    bias_upd = adamw_update(head_bias, bias_first, bias_second, bias_grad, small_rate)
    tile_sum = after(tile_sum, (embed_upd, position_upd, norm_upd, bias_upd, loss_value))
    tile_upd = tile_adamw(used, core_arr, state, tile_sum, over("ctx", tile_sum))
    return (loss_value, *tile_upd, *embed_upd, *position_upd, *norm_upd, *bias_upd)


def solution(mesh):
    grid = Mesh(mesh.devices.reshape(-1, 2, 2, 2), EVERY)
    halves, tiles, table = P("fsdp", "ctx"), P("fsdp", ("ty", "tx"), None), P("fsdp", None)
    norms, copied = P(None, None, "fsdp"), P()

    def three(spec):
        return (spec,) * 3

    return jax.shard_map(
        body,
        mesh=grid,
        in_specs=(halves, halves, copied, *three(tiles), *three(table), *three(table), *three(norms), *three(copied)),
        out_specs=(copied, *three(tiles), *three(table), *three(table), *three(norms), *three(copied)),
        check_vma=False,
    )
```

```python
import functools

import jax
import jax.numpy as jnp
from jax import lax
from jax.experimental import pallas as pl
from jax.experimental.pallas import tpu as pltpu
from jax.sharding import Mesh
from jax.sharding import PartitionSpec as P

HEAD_DIM = 48
VOCAB = 2025
LAYERS = 3
STEP = 10
TILES = 36
BLOCK = 256

norm_eps = 1e-05
beta_first = 0.9
beta_second = 0.999
learn_rate = 0.05
small_rate = 0.5
weight_decay = 0.01
adam_eps = 1e-08

bf16 = jnp.bfloat16
f32 = jnp.float32
FLIP = [(0, 1), (1, 0)]
PLANE = ("ctx", "ty", "tx")
EVERY = ("fsdp", "ctx", "ty", "tx")


def over(axis, v):
    return lax.ppermute(v, axis, FLIP)


def dot(left, right, dims):
    return lax.dot_general(left, right, (dims, ((), ())), preferred_element_type=f32)


def norm_parts(stream, gain, shift):
    centered = stream - jnp.mean(stream, -1, keepdims=True)
    inverse = lax.rsqrt(jnp.mean(centered * centered, -1, keepdims=True) + norm_eps)
    normal_hat = centered * inverse
    return (normal_hat * gain + shift, normal_hat, inverse)


def norm_back(gradient, normal_hat, inverse, gain):
    scaled = gradient * gain
    return inverse * (
        scaled
        - jnp.mean(scaled, -1, keepdims=True)
        - normal_hat * jnp.mean(scaled * normal_hat, -1, keepdims=True)
    )


def gelu_slope(pre_gelu):
    return (
        0.5 * (1.0 + lax.erf(pre_gelu * 0.7071067811865476))
        + pre_gelu * jnp.exp(-0.5 * pre_gelu * pre_gelu) * 0.3989422804014327
    )


def sum_over_x(partial):
    mine = partial.astype(bf16)
    return mine.astype(f32) + over("tx", mine).astype(f32)


def add_halves(keep, come):
    return (keep.astype(f32) + come.astype(f32)).astype(bf16)


def choose(bit, one, zero):
    return jnp.where(bit == 1, one, zero)


def both(axis, v, at, dim):
    other = over(axis, v)
    return lax.concatenate([choose(at, other, v), choose(at, v, other)], dim)


def after(value, event):
    return lax.optimization_barrier((value, event))[0]


def needs(value, event):
    first = lax.slice(event, (0,) * event.ndim, (1,) * event.ndim).reshape(())
    return value + jnp.minimum(jnp.abs(first), 0).astype(value.dtype)


def order_kernel(owner_ref, slot_ref, held_ref, out_ref, sem):
    def copy(t):
        return pltpu.make_async_copy(held_ref.at[owner_ref[t], :, slot_ref[t]], out_ref.at[t], sem.at[t])

    for t in range(out_ref.shape[0]):
        copy(t).start()
    for t in range(out_ref.shape[0]):
        copy(t).wait()


def order_tiles(held, owner, slot):
    count, (_, pieces, _, half, model) = owner.shape[0], held.shape
    scalar = pl.BlockSpec(memory_space=pltpu.SMEM)
    return pl.pallas_call(
        order_kernel,
        in_specs=[scalar, scalar, pl.BlockSpec(memory_space=pl.ANY)],
        out_specs=pl.BlockSpec(memory_space=pltpu.VMEM),
        out_shape=jax.ShapeDtypeStruct((count, pieces, half, model), bf16),
        scratch_shapes=[pltpu.SemaphoreType.DMA((count,))],
        compiler_params=pltpu.CompilerParams(vmem_limit_bytes=24 * 2**20),
        name="order_tiles",
    )(owner, slot, held)


def collect_kernel(count, owner_ref, slot_ref, *refs):
    sources, out_ref, sem = refs[:count], refs[-2], refs[-1]

    def copies():
        t = 0
        for source in sources:
            for i in range(source.shape[0]):
                yield pltpu.make_async_copy(source.at[i], out_ref.at[owner_ref[t], slot_ref[t]], sem.at[t])
                t += 1

    for copy in copies():
        copy.start()
    for copy in copies():
        copy.wait()


def collect(sources, owner, slot, n, slots, into=None):
    total, (half, model) = owner.shape[0], sources[0].shape[1:]
    scalar = pl.BlockSpec(memory_space=pltpu.SMEM)
    whole = pl.BlockSpec(memory_space=pltpu.VMEM)
    held = [] if into is None else [into]
    return pl.pallas_call(
        functools.partial(collect_kernel, len(sources)),
        in_specs=[scalar] * 2 + [whole] * len(sources) + [pl.BlockSpec(memory_space=pltpu.MemorySpace.HBM)] * len(held),
        out_specs=pl.BlockSpec(memory_space=pltpu.MemorySpace.HBM),
        out_shape=jax.ShapeDtypeStruct((n, slots, half, model), bf16),
        input_output_aliases={2 + len(sources): 0} if held else {},
        scratch_shapes=[pltpu.SemaphoreType.DMA((total,))],
        compiler_params=pltpu.CompilerParams(vmem_limit_bytes=58 * 2**20),
        name="collect",
    )(owner, slot, *sources, *held)


def attend_kernel(q_ref, *refs):
    kv_refs, (o_ref, total_ref) = refs[:-2], refs[-2:]
    scale = HEAD_DIM ** (-0.5)
    for i in range(q_ref.shape[0]):
        scores = [dot(kv[0, i], q_ref[i], ((0,), (0,))) * scale for kv in kv_refs]
        top = functools.reduce(jnp.maximum, [jnp.max(s, 0, keepdims=True) for s in scores])
        raised = [jnp.exp(s - top) for s in scores]
        total = sum(jnp.sum(e, 0, keepdims=True) for e in raised)
        share = 1.0 / total
        o_ref[i] = sum(
            dot(kv[1, i], (e * share).astype(bf16), ((1,), (0,))) for kv, e in zip(kv_refs, raised)
        ).astype(bf16)
        total_ref[i] = top + jnp.log(total)


def attend(queries, blocks):
    heads, size, rows = queries.shape
    step = 2
    short = pl.BlockSpec((step, size, rows), lambda h: (h, 0, 0))
    block = pl.BlockSpec((2, step, size, rows), lambda h: (0, h, 0, 0))
    return pl.pallas_call(
        attend_kernel,
        grid=(heads // step,),
        in_specs=[short] + [block] * len(blocks),
        out_specs=[short, pl.BlockSpec((step, 1, rows), lambda h: (h, 0, 0))],
        out_shape=[
            jax.ShapeDtypeStruct((heads, size, rows), bf16),
            jax.ShapeDtypeStruct((heads, 1, rows), f32),
        ],
        compiler_params=pltpu.CompilerParams(vmem_limit_bytes=32 * 2**20),
        name="attend",
    )(queries, *blocks)


def attend_back_kernel(count, q_ref, g_ref, total_ref, *refs):
    kv_refs, dq_ref, dkv_refs = refs[:count], refs[count], refs[count + 1:]
    scale = HEAD_DIM ** (-0.5)
    for i in range(q_ref.shape[0]):
        soft = [jnp.exp(dot(kv[0, i], q_ref[i], ((0,), (0,))) * scale - total_ref[i]) for kv in kv_refs]
        grad_soft = [dot(kv[1, i], g_ref[i], ((0,), (0,))) for kv in kv_refs]
        mean = sum(jnp.sum(p * g, 0, keepdims=True) for p, g in zip(soft, grad_soft))
        grad_scores = [(p * (g - mean)).astype(bf16) for p, g in zip(soft, grad_soft)]
        dq = sum(dot(kv[0, i], ds, ((1,), (0,))) for kv, ds in zip(kv_refs, grad_scores))
        dq_ref[i] = (dq * scale).astype(bf16)
        for dkv, p, ds in zip(dkv_refs, soft, grad_scores):
            dkv[0, i] = (dot(q_ref[i], ds, ((1,), (1,))) * scale).astype(bf16)
            dkv[1, i] = dot(g_ref[i], p.astype(bf16), ((1,), (1,))).astype(bf16)


def attend_back(queries, blocks, gradient, total):
    heads, size, rows = queries.shape
    step = 2
    short = pl.BlockSpec((step, size, rows), lambda h: (h, 0, 0))
    block = pl.BlockSpec((2, step, size, rows), lambda h: (0, h, 0, 0))
    return pl.pallas_call(
        functools.partial(attend_back_kernel, len(blocks)),
        grid=(heads // step,),
        in_specs=[short, short, pl.BlockSpec((step, 1, rows), lambda h: (h, 0, 0))] + [block] * len(blocks),
        out_specs=[short] + [block] * len(blocks),
        out_shape=[jax.ShapeDtypeStruct((heads, size, rows), bf16)]
        + [jax.ShapeDtypeStruct(kv.shape, bf16) for kv in blocks],
        compiler_params=pltpu.CompilerParams(vmem_limit_bytes=32 * 2**20),
        name="attend_back",
    )(queries, gradient, total, *blocks)


def adamw_update(weight, moment_one, moment_two, gradient, rate):
    moment_one = beta_first * moment_one + (1.0 - beta_first) * gradient
    moment_two = beta_second * moment_two + (1.0 - beta_second) * gradient * gradient
    first_hat = moment_one / (1.0 - beta_first**STEP)
    second_hat = moment_two / (1.0 - beta_second**STEP)
    weight = weight - rate * (first_hat / (jnp.sqrt(second_hat) + adam_eps) + weight_decay * weight)
    return (weight, moment_one, moment_two)


def tile_adamw_kernel(used_ref, core_ref, w_ref, m_ref, v_ref, own_ref, oth_ref, w_out, m_out, v_out):
    slot = pl.program_id(0)
    half = w_ref.shape[1] // 2

    @pl.when(used_ref[slot] == 1)
    def _():
        for h, g_ref in enumerate((own_ref, oth_ref)):
            side = core_ref[0] if h == 0 else 1 - core_ref[0]
            at = pl.ds(pl.multiple_of(side * half, half), half)
            new = adamw_update(w_ref[0, at], m_ref[0, at], v_ref[0, at], g_ref[0].astype(f32), learn_rate)
            w_out[0, at], m_out[0, at], v_out[0, at] = new

    @pl.when(used_ref[slot] != 1)
    def _():
        w_out[...], m_out[...], v_out[...] = w_ref[...], m_ref[...], v_ref[...]


def tile_adamw(used, core, state, own, oth):
    slots, rows, width = state[0].shape
    block = pl.BlockSpec((1, rows, width), lambda s, u, c: (s, 0, 0))
    grad_block = pl.BlockSpec((1, rows // 2, width), lambda s, u, c: (s, 0, 0))
    return pl.pallas_call(
        tile_adamw_kernel,
        grid_spec=pltpu.PrefetchScalarGridSpec(
            num_scalar_prefetch=2,
            grid=(slots,),
            in_specs=[block, block, block, grad_block, grad_block],
            out_specs=[block, block, block],
        ),
        out_shape=[jax.ShapeDtypeStruct(state[0].shape, f32)] * 3,
        compiler_params=pltpu.CompilerParams(vmem_limit_bytes=58 * 2**20),
        name="tile_adamw",
    )(used, core, *state, own, oth)


def body(
    token_ids,
    masked,
    tile_slot,
    tile_master,
    tile_first,
    tile_second,
    embedding,
    embed_first,
    embed_second,
    position_table,
    position_first,
    position_second,
    norm_params,
    norm_first,
    norm_second,
    head_bias,
    bias_first,
    bias_second,
):
    n = lax.axis_size("fsdp")
    z, core, ty, tx = (lax.axis_index(a) for a in EVERY)
    slots, width, model = tile_master.shape
    half = width // 2
    columns = 2 * width
    heads = columns // HEAD_DIM
    half_len = token_ids.shape[1]
    rows = half_len // 2
    share = rows // 2
    own_dim = embedding.shape[0]
    norms = norm_params.shape[1]
    core_arr = core.reshape(1).astype(jnp.int32)
    piece_at = core * 2 + ty

    owner = tile_slot // slots
    held = lax.dynamic_slice(tile_master, (0, core * half, 0), (slots, half, model)).astype(bf16)
    held = lax.all_gather(held, ("fsdp", "ctx", "ty"), axis=0, tiled=True).reshape(n, 4, slots, half, model)

    block_at = (core * 2 + tx) * 2 + ty
    vocab_pad = 8 * BLOCK - VOCAB
    wide = BLOCK + rows
    embed_pad = jnp.pad(embedding.astype(bf16), ((0, 0), (0, vocab_pad)))
    ids_half = jnp.where(masked == 1, VOCAB - 1, token_ids)
    ids = lax.dynamic_slice(ids_half, (0, ty * rows), (1, rows))
    coded = lax.dynamic_slice(ids_half * 2 + masked, (0, ty * rows), (1, rows))
    coded = jnp.concatenate([coded // 256, coded % 256], 1).astype(bf16)
    packed = jnp.concatenate(
        [
            lax.dynamic_slice(embed_pad, (0, block_at * BLOCK), (own_dim, BLOCK)),
            lax.dynamic_slice(position_table, (0, piece_at * rows), (own_dim, rows)).astype(bf16),
        ],
        1,
    )
    packed = jnp.concatenate(
        [
            packed,
            jnp.pad(norm_params.astype(bf16).reshape(2 * norms, own_dim), ((0, 0), (0, wide - own_dim))),
            jnp.pad(coded, ((0, 15 - 2 * norms), (0, wide - 2 * rows))),
        ],
        0,
    )
    tables = lax.all_gather(packed, "fsdp", axis=0)
    embed_all = tables[:, :own_dim, :BLOCK].reshape(model, BLOCK)
    for axis, at in (("ty", ty), ("tx", tx), ("ctx", core)):
        embed_all = both(axis, embed_all, at, 1)
    places_own = tables[:, :own_dim, BLOCK:].reshape(model, rows).T.astype(f32)
    gains = tables[:, own_dim:own_dim + 2 * norms, :own_dim].transpose(1, 0, 2)
    gains = gains.reshape(2, norms, model).astype(f32)
    coded = tables[:, own_dim + 2 * norms, :2 * rows].reshape(n, 1, 2, rows)
    for axis, at in (("ty", ty), ("ctx", core)):
        coded = both(axis, coded, at, 1)
    coded = coded.astype(f32).astype(jnp.int32)
    coded = coded[:, :, 0] * 256 + coded[:, :, 1]
    all_ids = coded // 2
    count = jnp.sum(coded % 2).astype(f32)
    column_at = lax.broadcasted_iota(jnp.int32, (1, 8 * BLOCK), 1)
    pick_ids = (ids.reshape(rows, 1) == column_at).astype(bf16)
    stream = dot(pick_ids, embed_all, ((1,), (1,))) + places_own

    weights, kept_layers = [], []
    for layer in range(LAYERS):
        mine = slice(12 * layer, 12 * layer + 12)
        tiles = order_tiles(held, owner[mine], tile_slot[mine] % slots).reshape(12 * columns, model)
        w_qkv, w_o = tiles[:3 * columns], tiles[3 * columns:4 * columns]
        w_in, w_out = tiles[4 * columns:8 * columns], tiles[8 * columns:]
        weights.append((w_qkv, w_o, w_in, w_out))
        normed = norm_parts(stream, gains[0, 2 * layer], gains[1, 2 * layer])[0].astype(bf16)
        kv = dot(w_qkv[columns:], normed, ((1,), (1,))).astype(bf16)
        kv_y = over("ty", kv)
        blocks = [kv, kv_y, over("ctx", kv), over("ctx", kv_y)]
        blocks = [block.reshape(2, heads, HEAD_DIM, rows) for block in blocks]
        queries = dot(w_qkv[:columns], normed, ((1,), (1,))).astype(bf16).reshape(heads, HEAD_DIM, rows)
        mixed, log_total = attend(queries, blocks)
        mixed = mixed.reshape(columns, rows)
        middle = stream + sum_over_x(dot(mixed, w_o, ((0,), (0,))))
        normed_mlp = norm_parts(middle, gains[0, 2 * layer + 1], gains[1, 2 * layer + 1])[0].astype(bf16)
        pre_gelu = dot(normed_mlp, w_in, ((1,), (1,)))
        activation = jax.nn.gelu(pre_gelu, approximate=False).astype(bf16)
        kept_layers.append((stream, middle, queries, blocks, log_total, mixed, pre_gelu))
        stream = middle + sum_over_x(dot(activation, w_out, ((1,), (0,))))

    final_rows = lax.dynamic_slice_in_dim(stream, tx * share, share, 0)
    final_normed, hat_final, inv_final = norm_parts(final_rows, gains[0, 2 * LAYERS], gains[1, 2 * LAYERS])
    final_normed = final_normed.astype(bf16)
    bias_row = jnp.pad(head_bias, (0, vocab_pad)).reshape(1, 8 * BLOCK)
    logits = dot(final_normed, embed_all, ((1,), (0,))) + bias_row
    logits = jnp.where(column_at < VOCAB, logits, -1e30)
    start = ty * rows + tx * share
    targets = lax.dynamic_slice(token_ids, (0, start), (1, share)).reshape(share, 1)
    row_weights = lax.dynamic_slice(masked, (0, start), (1, share)).reshape(share, 1).astype(f32)
    row_top = jnp.max(logits, -1, keepdims=True)
    log_total = row_top + jnp.log(jnp.sum(jnp.exp(logits - row_top), -1, keepdims=True))
    is_target = targets == column_at
    picked = jnp.sum(jnp.where(is_target, logits, 0.0), -1, keepdims=True)
    loss_part = jnp.sum((log_total - picked) * row_weights)
    grad_logits = (
        (jnp.exp(logits - log_total) - is_target.astype(f32)) * (row_weights / count)
    ).astype(bf16)
    bias_sum = jnp.sum(grad_logits.astype(f32), 0, keepdims=True)
    bias_sum = jnp.where(column_at == 8 * BLOCK - 1, loss_part, bias_sum)
    for axis in PLANE:
        bias_sum = bias_sum + over(axis, bias_sum)
    bit = 1
    while bit < n:
        bias_sum = bias_sum + lax.ppermute(bias_sum, "fsdp", [(i, i ^ bit) for i in range(n)])
        bit *= 2
    bias_grad = bias_sum[0, :VOCAB]
    loss_value = bias_sum[0, 8 * BLOCK - 1] / count
    grad_final = dot(grad_logits, embed_all, ((1,), (1,)))
    part = norm_back(grad_final, hat_final, inv_final, gains[0, 2 * LAYERS]).astype(bf16)
    gradient = both("tx", part, tx, 0).astype(f32)
    final_norm_grad = jnp.stack([jnp.sum(grad_final * hat_final, 0), jnp.sum(grad_final, 0)])
    final_norm_grad = final_norm_grad + over("tx", final_norm_grad)

    embed_part = dot(final_normed, grad_logits, ((0,), (0,))).astype(bf16)
    embed_part = lax.psum_scatter(embed_part, "fsdp", scatter_dimension=0, tiled=True)
    offloaded = [embed_part]
    for axis, at in (("ctx", core), ("tx", tx), ("ty", ty)):
        cut = embed_part.shape[1] // 2
        keep = lax.dynamic_slice_in_dim(embed_part, at * cut, cut, 1)
        send = lax.dynamic_slice_in_dim(embed_part, cut - at * cut, cut, 1)
        embed_part = add_halves(keep, over(axis, send))
    embed_head = embed_part
    for axis, at in (("ty", ty), ("tx", tx), ("ctx", core)):
        embed_head = both(axis, embed_head, at, 1)

    norm_grads = [None] * norms
    norm_grads[2 * LAYERS] = final_norm_grad
    tile_grads, tile_list = [], []

    def core_sum(grads):
        keep = lax.dynamic_slice_in_dim(grads, core * 2, 2, 1).astype(bf16)
        send = lax.dynamic_slice_in_dim(grads, 2 - core * 2, 2, 1).astype(bf16)
        return add_halves(keep, over("ctx", send)).transpose(1, 0, 2, 3)

    def neighbour_sum(two):
        keep = lax.dynamic_index_in_dim(two, ty, 0, False)
        send = lax.dynamic_index_in_dim(two, 1 - ty, 0, False)
        return add_halves(keep, over("ty", send))

    def offloaded_sum(flat, axis):
        flat = after(flat, offloaded[0]) if len(offloaded) == 1 else flat
        offloaded.append(lax.psum_scatter(flat, axis, scatter_dimension=0, tiled=True))
        return offloaded[-1]

    attn_two = None
    for layer in reversed(range(LAYERS)):
        stream, middle, queries, blocks, log_total, mixed, pre_gelu = kept_layers[layer]
        w_qkv, w_o, w_in, w_out = weights[layer]
        branch = gradient.astype(bf16)
        activation = jax.nn.gelu(pre_gelu, approximate=False).astype(bf16)
        grad_act = dot(branch, w_out, ((1,), (1,)))
        grad_pre = (grad_act * gelu_slope(pre_gelu)).astype(bf16)
        normed_mlp, hat_mlp, inv_mlp = norm_parts(middle, gains[0, 2 * layer + 1], gains[1, 2 * layer + 1])
        partial = dot(grad_pre, w_in, ((1,), (0,))).astype(bf16)
        grad_normed = sum_over_x(partial)
        grad_out = dot(needs(activation, partial), branch, ((0,), (0,))).reshape(4, 4, half, model)
        grad_in = dot(grad_pre, needs(normed_mlp.astype(bf16), partial), ((0,), (0,))).reshape(4, 4, half, model)
        two = core_sum(jnp.concatenate([grad_in, grad_out], 0))
        tile_list += range(12 * layer + 4, 12 * layer + 12)
        if attn_two is not None:
            two = jnp.concatenate([two, attn_two], 1)
            tile_list += range(12 * layer + 12, 12 * layer + 16)
        grad_middle = gradient + norm_back(grad_normed, hat_mlp, inv_mlp, gains[0, 2 * layer + 1])
        norm_grads[2 * layer + 1] = jnp.stack([jnp.sum(grad_normed * hat_mlp, 0), jnp.sum(grad_normed, 0)])
        branch = grad_middle.astype(bf16)
        grad_proj_out = dot(mixed, branch, ((1,), (0,)))
        grad_mixed = dot(w_o, branch, ((1,), (1,))).astype(bf16).reshape(heads, HEAD_DIM, rows)
        grad_queries, kv_own, kv_y, kv_core, kv_both = attend_back(queries, blocks, grad_mixed, log_total)
        kv_own = kv_own.astype(f32) + over("ctx", kv_core).astype(f32)
        from_y = over("ty", add_halves(kv_y, over("ctx", kv_both)))
        grad_kv = (kv_own + from_y.astype(f32)).astype(bf16).reshape(2 * columns, rows)
        two = needs(two, from_y) if layer else two
        tile_grads.append(offloaded_sum(two.reshape(-1, half, model), "ty"))
        grad_qkv = jnp.concatenate([grad_queries.reshape(columns, rows), grad_kv], 0)
        normed, hat_attn, inv_attn = norm_parts(stream, gains[0, 2 * layer], gains[1, 2 * layer])
        partial = dot(grad_qkv, w_qkv, ((0,), (0,))).astype(bf16)
        grad_normed = sum_over_x(partial)
        grad_w = dot(grad_qkv, needs(normed.astype(bf16), partial), ((1,), (0,)))
        grad_w = jnp.concatenate([grad_w, grad_proj_out], 0).reshape(4, 4, half, model)
        attn_two = core_sum(grad_w)
        gradient = grad_middle + norm_back(grad_normed, hat_attn, inv_attn, gains[0, 2 * layer])
        norm_grads[2 * layer] = jnp.stack([jnp.sum(grad_normed * hat_attn, 0), jnp.sum(grad_normed, 0)])

    norm_rows = jnp.stack(norm_grads, 1).reshape(2 * norms, model)
    state = jnp.concatenate(
        [gradient.astype(bf16), norm_rows.astype(bf16), jnp.zeros((16 - 2 * norms, model), bf16)], 0
    )
    state = state.reshape(rows + 16, n, own_dim).transpose(1, 0, 2)
    state = lax.all_to_all(state, "fsdp", 0, 0)[:, None]
    last_grads = needs(neighbour_sum(attn_two), state)
    state = both("ty", state, ty, 1)
    state = both("ctx", state, core, 1)
    norm_grad = jnp.sum(state[:, :, rows:rows + 2 * norms].astype(f32), (0, 1)).reshape(2, norms, own_dim)
    token_grads = state[:, :, :rows]
    position_grad = jnp.sum(token_grads.astype(f32), 0).reshape(4 * rows, own_dim).T
    picks = (all_ids.reshape(n * 4 * rows, 1) == column_at).astype(bf16)
    embed_tail = dot(token_grads.reshape(n * 4 * rows, own_dim), picks, ((0,), (0,)))
    embed_grad = (embed_tail + embed_head.astype(f32))[:, :VOCAB]

    at = jnp.array(tile_list, jnp.int32)
    sent = collect(tile_grads, owner[at], tile_slot[at] % slots, n, slots)
    sent = collect([last_grads], owner[:4], tile_slot[:4] % slots, n, slots, sent)
    tile_sum = offloaded_sum(sent.reshape(-1, half, model), "fsdp")
    used = jnp.any((tile_slot - z * slots)[None, :] == jnp.arange(slots, dtype=jnp.int32)[:, None], 1).astype(jnp.int32)
    state = (tile_master, tile_first, tile_second)
    embed_upd = adamw_update(embedding, embed_first, embed_second, embed_grad, learn_rate)
    position_upd = adamw_update(position_table, position_first, position_second, position_grad, learn_rate)
    norm_upd = adamw_update(norm_params, norm_first, norm_second, norm_grad, small_rate)
    bias_upd = adamw_update(head_bias, bias_first, bias_second, bias_grad, small_rate)
    tile_sum = after(tile_sum, (embed_upd, position_upd, norm_upd, bias_upd, loss_value))
    tile_upd = tile_adamw(used, core_arr, state, tile_sum, over("ctx", tile_sum))
    return (loss_value, *tile_upd, *embed_upd, *position_upd, *norm_upd, *bias_upd)


def solution(mesh):
    grid = Mesh(mesh.devices.reshape(-1, 2, 2, 2), EVERY)
    halves, tiles, table = P("fsdp", "ctx"), P("fsdp", ("ty", "tx"), None), P("fsdp", None)
    norms, copied = P(None, None, "fsdp"), P()

    def three(spec):
        return (spec,) * 3

    return jax.shard_map(
        body,
        mesh=grid,
        in_specs=(halves, halves, copied, *three(tiles), *three(table), *three(table), *three(norms), *three(copied)),
        out_specs=(copied, *three(tiles), *three(table), *three(table), *three(norms), *three(copied)),
        check_vma=False,
    )
```

```python
import functools

import jax
import jax.numpy as jnp
from jax import lax
from jax.experimental import pallas as pl
from jax.experimental.pallas import tpu as pltpu
from jax.sharding import Mesh
from jax.sharding import PartitionSpec as P

HEAD_DIM = 48
VOCAB = 2025
LAYERS = 3
STEP = 10
TILES = 36
BLOCK = 256

norm_eps = 1e-05
beta_first = 0.9
beta_second = 0.999
learn_rate = 0.05
small_rate = 0.5
weight_decay = 0.01
adam_eps = 1e-08

bf16 = jnp.bfloat16
f32 = jnp.float32
FLIP = [(0, 1), (1, 0)]
PLANE = ("ctx", "ty", "tx")
EVERY = ("fsdp", "ctx", "ty", "tx")


def over(axis, v):
    return lax.ppermute(v, axis, FLIP)


def dot(left, right, dims):
    return lax.dot_general(left, right, (dims, ((), ())), preferred_element_type=f32)


def norm_parts(stream, gain, shift):
    centered = stream - jnp.mean(stream, -1, keepdims=True)
    inverse = lax.rsqrt(jnp.mean(centered * centered, -1, keepdims=True) + norm_eps)
    normal_hat = centered * inverse
    return (normal_hat * gain + shift, normal_hat, inverse)


def norm_back(gradient, normal_hat, inverse, gain):
    scaled = gradient * gain
    return inverse * (
        scaled
        - jnp.mean(scaled, -1, keepdims=True)
        - normal_hat * jnp.mean(scaled * normal_hat, -1, keepdims=True)
    )


def gelu_slope(pre_gelu):
    return (
        0.5 * (1.0 + lax.erf(pre_gelu * 0.7071067811865476))
        + pre_gelu * jnp.exp(-0.5 * pre_gelu * pre_gelu) * 0.3989422804014327
    )


def sum_over_x(partial):
    mine = partial.astype(bf16)
    return mine.astype(f32) + over("tx", mine).astype(f32)


def add_halves(keep, come):
    return (keep.astype(f32) + come.astype(f32)).astype(bf16)


def choose(bit, one, zero):
    return jnp.where(bit == 1, one, zero)


def both(axis, v, at, dim):
    other = over(axis, v)
    return lax.concatenate([choose(at, other, v), choose(at, v, other)], dim)


def after(value, event):
    return lax.optimization_barrier((value, event))[0]


def needs(value, event):
    first = lax.slice(event, (0,) * event.ndim, (1,) * event.ndim).reshape(())
    return value + jnp.minimum(jnp.abs(first), 0).astype(value.dtype)


def order_kernel(owner_ref, slot_ref, held_ref, out_ref, sem):
    def copy(t):
        return pltpu.make_async_copy(held_ref.at[owner_ref[t], :, slot_ref[t]], out_ref.at[t], sem.at[t])

    for t in range(out_ref.shape[0]):
        copy(t).start()
    for t in range(out_ref.shape[0]):
        copy(t).wait()


def order_tiles(held, owner, slot):
    count, (_, pieces, _, half, model) = owner.shape[0], held.shape
    scalar = pl.BlockSpec(memory_space=pltpu.SMEM)
    return pl.pallas_call(
        order_kernel,
        in_specs=[scalar, scalar, pl.BlockSpec(memory_space=pl.ANY)],
        out_specs=pl.BlockSpec(memory_space=pltpu.VMEM),
        out_shape=jax.ShapeDtypeStruct((count, pieces, half, model), bf16),
        scratch_shapes=[pltpu.SemaphoreType.DMA((count,))],
        compiler_params=pltpu.CompilerParams(vmem_limit_bytes=24 * 2**20),
        name="order_tiles",
    )(owner, slot, held)


def collect_kernel(count, owner_ref, slot_ref, *refs):
    sources, out_ref, sem = refs[:count], refs[-2], refs[-1]

    def copies():
        t = 0
        for source in sources:
            for i in range(source.shape[0]):
                yield pltpu.make_async_copy(source.at[i], out_ref.at[owner_ref[t], slot_ref[t]], sem.at[t])
                t += 1

    for copy in copies():
        copy.start()
    for copy in copies():
        copy.wait()


def collect(sources, owner, slot, n, slots, into=None):
    total, (half, model) = owner.shape[0], sources[0].shape[1:]
    scalar = pl.BlockSpec(memory_space=pltpu.SMEM)
    whole = pl.BlockSpec(memory_space=pltpu.VMEM)
    held = [] if into is None else [into]
    return pl.pallas_call(
        functools.partial(collect_kernel, len(sources)),
        in_specs=[scalar] * 2 + [whole] * len(sources) + [pl.BlockSpec(memory_space=pltpu.MemorySpace.HBM)] * len(held),
        out_specs=pl.BlockSpec(memory_space=pltpu.MemorySpace.HBM),
        out_shape=jax.ShapeDtypeStruct((n, slots, half, model), bf16),
        input_output_aliases={2 + len(sources): 0} if held else {},
        scratch_shapes=[pltpu.SemaphoreType.DMA((total,))],
        compiler_params=pltpu.CompilerParams(vmem_limit_bytes=58 * 2**20),
        name="collect",
    )(owner, slot, *sources, *held)


def attend_kernel(q_ref, *refs):
    kv_refs, (o_ref, total_ref) = refs[:-2], refs[-2:]
    scale = HEAD_DIM ** (-0.5)
    for i in range(q_ref.shape[0]):
        scores = [dot(kv[0, i], q_ref[i], ((0,), (0,))) * scale for kv in kv_refs]
        top = functools.reduce(jnp.maximum, [jnp.max(s, 0, keepdims=True) for s in scores])
        raised = [jnp.exp(s - top) for s in scores]
        total = sum(jnp.sum(e, 0, keepdims=True) for e in raised)
        share = 1.0 / total
        o_ref[i] = sum(
            dot(kv[1, i], (e * share).astype(bf16), ((1,), (0,))) for kv, e in zip(kv_refs, raised)
        ).astype(bf16)
        total_ref[i] = top + jnp.log(total)


def attend(queries, blocks):
    heads, size, rows = queries.shape
    step = 2
    short = pl.BlockSpec((step, size, rows), lambda h: (h, 0, 0))
    block = pl.BlockSpec((2, step, size, rows), lambda h: (0, h, 0, 0))
    return pl.pallas_call(
        attend_kernel,
        grid=(heads // step,),
        in_specs=[short] + [block] * len(blocks),
        out_specs=[short, pl.BlockSpec((step, 1, rows), lambda h: (h, 0, 0))],
        out_shape=[
            jax.ShapeDtypeStruct((heads, size, rows), bf16),
            jax.ShapeDtypeStruct((heads, 1, rows), f32),
        ],
        compiler_params=pltpu.CompilerParams(vmem_limit_bytes=32 * 2**20),
        name="attend",
    )(queries, *blocks)


def attend_back_kernel(count, q_ref, g_ref, total_ref, *refs):
    kv_refs, dq_ref, dkv_refs = refs[:count], refs[count], refs[count + 1:]
    scale = HEAD_DIM ** (-0.5)
    for i in range(q_ref.shape[0]):
        soft = [jnp.exp(dot(kv[0, i], q_ref[i], ((0,), (0,))) * scale - total_ref[i]) for kv in kv_refs]
        grad_soft = [dot(kv[1, i], g_ref[i], ((0,), (0,))) for kv in kv_refs]
        mean = sum(jnp.sum(p * g, 0, keepdims=True) for p, g in zip(soft, grad_soft))
        grad_scores = [(p * (g - mean)).astype(bf16) for p, g in zip(soft, grad_soft)]
        dq = sum(dot(kv[0, i], ds, ((1,), (0,))) for kv, ds in zip(kv_refs, grad_scores))
        dq_ref[i] = (dq * scale).astype(bf16)
        for dkv, p, ds in zip(dkv_refs, soft, grad_scores):
            dkv[0, i] = (dot(q_ref[i], ds, ((1,), (1,))) * scale).astype(bf16)
            dkv[1, i] = dot(g_ref[i], p.astype(bf16), ((1,), (1,))).astype(bf16)


def attend_back(queries, blocks, gradient, total):
    heads, size, rows = queries.shape
    step = 2
    short = pl.BlockSpec((step, size, rows), lambda h: (h, 0, 0))
    block = pl.BlockSpec((2, step, size, rows), lambda h: (0, h, 0, 0))
    return pl.pallas_call(
        functools.partial(attend_back_kernel, len(blocks)),
        grid=(heads // step,),
        in_specs=[short, short, pl.BlockSpec((step, 1, rows), lambda h: (h, 0, 0))] + [block] * len(blocks),
        out_specs=[short] + [block] * len(blocks),
        out_shape=[jax.ShapeDtypeStruct((heads, size, rows), bf16)]
        + [jax.ShapeDtypeStruct(kv.shape, bf16) for kv in blocks],
        compiler_params=pltpu.CompilerParams(vmem_limit_bytes=32 * 2**20),
        name="attend_back",
    )(queries, gradient, total, *blocks)


def adamw_update(weight, moment_one, moment_two, gradient, rate):
    moment_one = beta_first * moment_one + (1.0 - beta_first) * gradient
    moment_two = beta_second * moment_two + (1.0 - beta_second) * gradient * gradient
    first_hat = moment_one * (1.0 / (1.0 - beta_first**STEP))
    second_hat = moment_two * (1.0 / (1.0 - beta_second**STEP))
    weight = weight - rate * (first_hat / (jnp.sqrt(second_hat) + adam_eps) + weight_decay * weight)
    return (weight, moment_one, moment_two)


def tile_adamw_kernel(used_ref, core_ref, w_ref, m_ref, v_ref, own_ref, oth_ref, w_out, m_out, v_out):
    slot = pl.program_id(0)
    half = w_ref.shape[1] // 2

    @pl.when(used_ref[slot] == 1)
    def _():
        for h, g_ref in enumerate((own_ref, oth_ref)):
            side = core_ref[0] if h == 0 else 1 - core_ref[0]
            at = pl.ds(pl.multiple_of(side * half, half), half)
            new = adamw_update(w_ref[0, at], m_ref[0, at], v_ref[0, at], g_ref[0].astype(f32), learn_rate)
            w_out[0, at], m_out[0, at], v_out[0, at] = new

    @pl.when(used_ref[slot] != 1)
    def _():
        w_out[...], m_out[...], v_out[...] = w_ref[...], m_ref[...], v_ref[...]


def tile_adamw(used, core, state, own, oth):
    slots, rows, width = state[0].shape
    block = pl.BlockSpec((1, rows, width), lambda s, u, c: (s, 0, 0))
    grad_block = pl.BlockSpec((1, rows // 2, width), lambda s, u, c: (s, 0, 0))
    return pl.pallas_call(
        tile_adamw_kernel,
        grid_spec=pltpu.PrefetchScalarGridSpec(
            num_scalar_prefetch=2,
            grid=(slots,),
            in_specs=[block, block, block, grad_block, grad_block],
            out_specs=[block, block, block],
        ),
        out_shape=[jax.ShapeDtypeStruct(state[0].shape, f32)] * 3,
        compiler_params=pltpu.CompilerParams(vmem_limit_bytes=58 * 2**20),
        name="tile_adamw",
    )(used, core, *state, own, oth)


def body(
    token_ids,
    masked,
    tile_slot,
    tile_master,
    tile_first,
    tile_second,
    embedding,
    embed_first,
    embed_second,
    position_table,
    position_first,
    position_second,
    norm_params,
    norm_first,
    norm_second,
    head_bias,
    bias_first,
    bias_second,
):
    n = lax.axis_size("fsdp")
    z, core, ty, tx = (lax.axis_index(a) for a in EVERY)
    slots, width, model = tile_master.shape
    half = width // 2
    columns = 2 * width
    heads = columns // HEAD_DIM
    half_len = token_ids.shape[1]
    rows = half_len // 2
    share = rows // 2
    own_dim = embedding.shape[0]
    norms = norm_params.shape[1]
    core_arr = core.reshape(1).astype(jnp.int32)
    piece_at = core * 2 + ty

    owner = tile_slot // slots
    held = lax.dynamic_slice(tile_master, (0, core * half, 0), (slots, half, model)).astype(bf16)
    held = lax.all_gather(held, ("fsdp", "ctx", "ty"), axis=0, tiled=True).reshape(n, 4, slots, half, model)

    block_at = (core * 2 + tx) * 2 + ty
    vocab_pad = 8 * BLOCK - VOCAB
    wide = BLOCK + rows
    embed_pad = jnp.pad(embedding.astype(bf16), ((0, 0), (0, vocab_pad)))
    ids_half = jnp.where(masked == 1, VOCAB - 1, token_ids)
    ids = lax.dynamic_slice(ids_half, (0, ty * rows), (1, rows))
    coded = lax.dynamic_slice(ids_half * 2 + masked, (0, ty * rows), (1, rows))
    coded = jnp.concatenate([coded // 256, coded % 256], 1).astype(bf16)
    packed = jnp.concatenate(
        [
            lax.dynamic_slice(embed_pad, (0, block_at * BLOCK), (own_dim, BLOCK)),
            lax.dynamic_slice(position_table, (0, piece_at * rows), (own_dim, rows)).astype(bf16),
        ],
        1,
    )
    packed = jnp.concatenate(
        [
            packed,
            jnp.pad(norm_params.astype(bf16).reshape(2 * norms, own_dim), ((0, 0), (0, wide - own_dim))),
            jnp.pad(coded, ((0, 15 - 2 * norms), (0, wide - 2 * rows))),
        ],
        0,
    )
    tables = lax.all_gather(packed, "fsdp", axis=0)
    embed_all = tables[:, :own_dim, :BLOCK].reshape(model, BLOCK)
    for axis, at in (("ty", ty), ("tx", tx), ("ctx", core)):
        embed_all = both(axis, embed_all, at, 1)
    places_own = tables[:, :own_dim, BLOCK:].reshape(model, rows).T.astype(f32)
    gains = tables[:, own_dim:own_dim + 2 * norms, :own_dim].transpose(1, 0, 2)
    gains = gains.reshape(2, norms, model).astype(f32)
    coded = tables[:, own_dim + 2 * norms, :2 * rows].reshape(n, 1, 2, rows)
    for axis, at in (("ty", ty), ("ctx", core)):
        coded = both(axis, coded, at, 1)
    coded = coded.astype(f32).astype(jnp.int32)
    coded = coded[:, :, 0] * 256 + coded[:, :, 1]
    all_ids = coded // 2
    count = jnp.sum(coded % 2).astype(f32)
    column_at = lax.broadcasted_iota(jnp.int32, (1, 8 * BLOCK), 1)
    pick_ids = (ids.reshape(rows, 1) == column_at).astype(bf16)
    stream = dot(pick_ids, embed_all, ((1,), (1,))) + places_own

    weights, kept_layers = [], []
    for layer in range(LAYERS):
        mine = slice(12 * layer, 12 * layer + 12)
        tiles = order_tiles(held, owner[mine], tile_slot[mine] % slots).reshape(12 * columns, model)
        w_qkv, w_o = tiles[:3 * columns], tiles[3 * columns:4 * columns]
        w_in, w_out = tiles[4 * columns:8 * columns], tiles[8 * columns:]
        weights.append((w_qkv, w_o, w_in, w_out))
        normed = norm_parts(stream, gains[0, 2 * layer], gains[1, 2 * layer])[0].astype(bf16)
        kv = dot(w_qkv[columns:], normed, ((1,), (1,))).astype(bf16)
        kv_y = over("ty", kv)
        blocks = [kv, kv_y, over("ctx", kv), over("ctx", kv_y)]
        blocks = [block.reshape(2, heads, HEAD_DIM, rows) for block in blocks]
        queries = dot(w_qkv[:columns], normed, ((1,), (1,))).astype(bf16).reshape(heads, HEAD_DIM, rows)
        mixed, log_total = attend(queries, blocks)
        mixed = mixed.reshape(columns, rows)
        middle = stream + sum_over_x(dot(mixed, w_o, ((0,), (0,))))
        normed_mlp = norm_parts(middle, gains[0, 2 * layer + 1], gains[1, 2 * layer + 1])[0].astype(bf16)
        pre_gelu = dot(normed_mlp, w_in, ((1,), (1,)))
        activation = jax.nn.gelu(pre_gelu, approximate=False).astype(bf16)
        kept_layers.append((stream, middle, queries, blocks, log_total, mixed, pre_gelu))
        stream = middle + sum_over_x(dot(activation, w_out, ((1,), (0,))))

    final_rows = lax.dynamic_slice_in_dim(stream, tx * share, share, 0)
    final_normed, hat_final, inv_final = norm_parts(final_rows, gains[0, 2 * LAYERS], gains[1, 2 * LAYERS])
    final_normed = final_normed.astype(bf16)
    bias_row = jnp.pad(head_bias, (0, vocab_pad)).reshape(1, 8 * BLOCK)
    logits = dot(final_normed, embed_all, ((1,), (0,))) + bias_row
    logits = jnp.where(column_at < VOCAB, logits, -1e30)
    start = ty * rows + tx * share
    targets = lax.dynamic_slice(token_ids, (0, start), (1, share)).reshape(share, 1)
    row_weights = lax.dynamic_slice(masked, (0, start), (1, share)).reshape(share, 1).astype(f32)
    row_top = jnp.max(logits, -1, keepdims=True)
    log_total = row_top + jnp.log(jnp.sum(jnp.exp(logits - row_top), -1, keepdims=True))
    is_target = targets == column_at
    picked = jnp.sum(jnp.where(is_target, logits, 0.0), -1, keepdims=True)
    loss_part = jnp.sum((log_total - picked) * row_weights)
    grad_logits = (
        (jnp.exp(logits - log_total) - is_target.astype(f32)) * (row_weights / count)
    ).astype(bf16)
    bias_sum = jnp.sum(grad_logits.astype(f32), 0, keepdims=True)
    bias_sum = jnp.where(column_at == 8 * BLOCK - 1, loss_part, bias_sum)
    for axis in PLANE:
        bias_sum = bias_sum + over(axis, bias_sum)
    bit = 1
    while bit < n:
        bias_sum = bias_sum + lax.ppermute(bias_sum, "fsdp", [(i, i ^ bit) for i in range(n)])
        bit *= 2
    bias_grad = bias_sum[0, :VOCAB]
    loss_value = bias_sum[0, 8 * BLOCK - 1] / count
    grad_final = dot(grad_logits, embed_all, ((1,), (1,)))
    part = norm_back(grad_final, hat_final, inv_final, gains[0, 2 * LAYERS]).astype(bf16)
    gradient = both("tx", part, tx, 0).astype(f32)
    final_norm_grad = jnp.stack([jnp.sum(grad_final * hat_final, 0), jnp.sum(grad_final, 0)])
    final_norm_grad = final_norm_grad + over("tx", final_norm_grad)

    embed_part = dot(final_normed, grad_logits, ((0,), (0,))).astype(bf16)
    embed_part = lax.psum_scatter(embed_part, "fsdp", scatter_dimension=0, tiled=True)
    offloaded = [embed_part]
    for axis, at in (("ctx", core), ("tx", tx), ("ty", ty)):
        cut = embed_part.shape[1] // 2
        keep = lax.dynamic_slice_in_dim(embed_part, at * cut, cut, 1)
        send = lax.dynamic_slice_in_dim(embed_part, cut - at * cut, cut, 1)
        embed_part = add_halves(keep, over(axis, send))
    embed_head = embed_part
    for axis, at in (("ty", ty), ("tx", tx), ("ctx", core)):
        embed_head = both(axis, embed_head, at, 1)

    norm_grads = [None] * norms
    norm_grads[2 * LAYERS] = final_norm_grad
    tile_grads, tile_list = [], []

    def core_sum(grads):
        keep = lax.dynamic_slice_in_dim(grads, core * 2, 2, 1).astype(bf16)
        send = lax.dynamic_slice_in_dim(grads, 2 - core * 2, 2, 1).astype(bf16)
        return add_halves(keep, over("ctx", send)).transpose(1, 0, 2, 3)

    def neighbour_sum(two):
        keep = lax.dynamic_index_in_dim(two, ty, 0, False)
        send = lax.dynamic_index_in_dim(two, 1 - ty, 0, False)
        return add_halves(keep, over("ty", send))

    def offloaded_sum(flat, axis):
        flat = after(flat, offloaded[0]) if len(offloaded) == 1 else flat
        offloaded.append(lax.psum_scatter(flat, axis, scatter_dimension=0, tiled=True))
        return offloaded[-1]

    attn_two = None
    for layer in reversed(range(LAYERS)):
        stream, middle, queries, blocks, log_total, mixed, pre_gelu = kept_layers[layer]
        w_qkv, w_o, w_in, w_out = weights[layer]
        branch = gradient.astype(bf16)
        activation = jax.nn.gelu(pre_gelu, approximate=False).astype(bf16)
        grad_act = dot(branch, w_out, ((1,), (1,)))
        grad_pre = (grad_act * gelu_slope(pre_gelu)).astype(bf16)
        normed_mlp, hat_mlp, inv_mlp = norm_parts(middle, gains[0, 2 * layer + 1], gains[1, 2 * layer + 1])
        partial = dot(grad_pre, w_in, ((1,), (0,))).astype(bf16)
        grad_normed = sum_over_x(partial)
        grad_out = dot(needs(activation, partial), branch, ((0,), (0,))).reshape(4, 4, half, model)
        grad_in = dot(grad_pre, needs(normed_mlp.astype(bf16), partial), ((0,), (0,))).reshape(4, 4, half, model)
        two = core_sum(jnp.concatenate([grad_in, grad_out], 0))
        tile_list += range(12 * layer + 4, 12 * layer + 12)
        if attn_two is not None:
            two = jnp.concatenate([two, attn_two], 1)
            tile_list += range(12 * layer + 12, 12 * layer + 16)
        grad_middle = gradient + norm_back(grad_normed, hat_mlp, inv_mlp, gains[0, 2 * layer + 1])
        norm_grads[2 * layer + 1] = jnp.stack([jnp.sum(grad_normed * hat_mlp, 0), jnp.sum(grad_normed, 0)])
        branch = grad_middle.astype(bf16)
        grad_proj_out = dot(mixed, branch, ((1,), (0,)))
        grad_mixed = dot(w_o, branch, ((1,), (1,))).astype(bf16).reshape(heads, HEAD_DIM, rows)
        grad_queries, kv_own, kv_y, kv_core, kv_both = attend_back(queries, blocks, grad_mixed, log_total)
        kv_own = kv_own.astype(f32) + over("ctx", kv_core).astype(f32)
        from_y = over("ty", add_halves(kv_y, over("ctx", kv_both)))
        grad_kv = (kv_own + from_y.astype(f32)).astype(bf16).reshape(2 * columns, rows)
        two = needs(two, from_y) if layer else two
        tile_grads.append(offloaded_sum(two.reshape(-1, half, model), "ty"))
        grad_qkv = jnp.concatenate([grad_queries.reshape(columns, rows), grad_kv], 0)
        normed, hat_attn, inv_attn = norm_parts(stream, gains[0, 2 * layer], gains[1, 2 * layer])
        partial = dot(grad_qkv, w_qkv, ((0,), (0,))).astype(bf16)
        grad_normed = sum_over_x(partial)
        grad_w = dot(grad_qkv, needs(normed.astype(bf16), partial), ((1,), (0,)))
        grad_w = jnp.concatenate([grad_w, grad_proj_out], 0).reshape(4, 4, half, model)
        attn_two = core_sum(grad_w)
        gradient = grad_middle + norm_back(grad_normed, hat_attn, inv_attn, gains[0, 2 * layer])
        norm_grads[2 * layer] = jnp.stack([jnp.sum(grad_normed * hat_attn, 0), jnp.sum(grad_normed, 0)])

    norm_rows = jnp.stack(norm_grads, 1).reshape(2 * norms, model)
    state = jnp.concatenate(
        [gradient.astype(bf16), norm_rows.astype(bf16), jnp.zeros((16 - 2 * norms, model), bf16)], 0
    )
    state = state.reshape(rows + 16, n, own_dim).transpose(1, 0, 2)
    state = lax.all_to_all(state, "fsdp", 0, 0)[:, None]
    last_grads = needs(neighbour_sum(attn_two), state)
    state = both("ty", state, ty, 1)
    state = both("ctx", state, core, 1)
    norm_grad = jnp.sum(state[:, :, rows:rows + 2 * norms].astype(f32), (0, 1)).reshape(2, norms, own_dim)
    token_grads = state[:, :, :rows]
    position_grad = jnp.sum(token_grads.astype(f32), 0).reshape(4 * rows, own_dim).T
    picks = (all_ids.reshape(n * 4 * rows, 1) == column_at).astype(bf16)
    embed_tail = dot(token_grads.reshape(n * 4 * rows, own_dim), picks, ((0,), (0,)))
    embed_grad = (embed_tail + embed_head.astype(f32))[:, :VOCAB]

    at = jnp.array(tile_list, jnp.int32)
    sent = collect(tile_grads, owner[at], tile_slot[at] % slots, n, slots)
    sent = collect([last_grads], owner[:4], tile_slot[:4] % slots, n, slots, sent)
    tile_sum = offloaded_sum(sent.reshape(-1, half, model), "fsdp")
    used = jnp.any((tile_slot - z * slots)[None, :] == jnp.arange(slots, dtype=jnp.int32)[:, None], 1).astype(jnp.int32)
    state = (tile_master, tile_first, tile_second)
    embed_upd = adamw_update(embedding, embed_first, embed_second, embed_grad, learn_rate)
    position_upd = adamw_update(position_table, position_first, position_second, position_grad, learn_rate)
    norm_upd = adamw_update(norm_params, norm_first, norm_second, norm_grad, small_rate)
    bias_upd = adamw_update(head_bias, bias_first, bias_second, bias_grad, small_rate)
    tile_sum = after(tile_sum, (embed_upd, position_upd, norm_upd, bias_upd, loss_value))
    tile_upd = tile_adamw(used, core_arr, state, tile_sum, over("ctx", tile_sum))
    return (loss_value, *tile_upd, *embed_upd, *position_upd, *norm_upd, *bias_upd)


def solution(mesh):
    grid = Mesh(mesh.devices.reshape(-1, 2, 2, 2), EVERY)
    halves, tiles, table = P("fsdp", "ctx"), P("fsdp", ("ty", "tx"), None), P("fsdp", None)
    norms, copied = P(None, None, "fsdp"), P()

    def three(spec):
        return (spec,) * 3

    return jax.shard_map(
        body,
        mesh=grid,
        in_specs=(halves, halves, copied, *three(tiles), *three(table), *three(table), *three(norms), *three(copied)),
        out_specs=(copied, *three(tiles), *three(table), *three(table), *three(norms), *three(copied)),
        check_vma=False,
    )
```

```python
import functools

import jax
import jax.numpy as jnp
from jax import lax
from jax.experimental import pallas as pl
from jax.experimental.pallas import tpu as pltpu
from jax.sharding import Mesh
from jax.sharding import PartitionSpec as P

HEAD_DIM = 48
VOCAB = 2025
LAYERS = 3
STEP = 10
TILES = 36
BLOCK = 256

norm_eps = 1e-05
beta_first = 0.9
beta_second = 0.999
learn_rate = 0.05
small_rate = 0.5
weight_decay = 0.01
adam_eps = 1e-08

bf16 = jnp.bfloat16
f32 = jnp.float32
FLIP = [(0, 1), (1, 0)]
PLANE = ("ctx", "ty", "tx")
EVERY = ("fsdp", "ctx", "ty", "tx")


def over(axis, v):
    return lax.ppermute(v, axis, FLIP)


def dot(left, right, dims):
    return lax.dot_general(left, right, (dims, ((), ())), preferred_element_type=f32)


def norm_parts(stream, gain, shift):
    centered = stream - jnp.mean(stream, -1, keepdims=True)
    inverse = lax.rsqrt(jnp.mean(centered * centered, -1, keepdims=True) + norm_eps)
    normal_hat = centered * inverse
    return (normal_hat * gain + shift, normal_hat, inverse)


def norm_back(gradient, normal_hat, inverse, gain):
    scaled = gradient * gain
    return inverse * (
        scaled
        - jnp.mean(scaled, -1, keepdims=True)
        - normal_hat * jnp.mean(scaled * normal_hat, -1, keepdims=True)
    )


def gelu_slope(pre_gelu):
    return (
        0.5 * (1.0 + lax.erf(pre_gelu * 0.7071067811865476))
        + pre_gelu * jnp.exp(-0.5 * pre_gelu * pre_gelu) * 0.3989422804014327
    )


def sum_over_x(partial):
    mine = partial.astype(bf16)
    return mine.astype(f32) + over("tx", mine).astype(f32)


def add_halves(keep, come):
    return (keep.astype(f32) + come.astype(f32)).astype(bf16)


def choose(bit, one, zero):
    return jnp.where(bit == 1, one, zero)


def both(axis, v, at, dim):
    other = over(axis, v)
    return lax.concatenate([choose(at, other, v), choose(at, v, other)], dim)


def after(value, event):
    return lax.optimization_barrier((value, event))[0]


def needs(value, event):
    first = lax.slice(event, (0,) * event.ndim, (1,) * event.ndim).reshape(())
    return value + jnp.minimum(jnp.abs(first), 0).astype(value.dtype)


def order_kernel(owner_ref, slot_ref, held_ref, out_ref, sem):
    def copy(t):
        return pltpu.make_async_copy(held_ref.at[owner_ref[t], :, slot_ref[t]], out_ref.at[t], sem.at[t])

    for t in range(out_ref.shape[0]):
        copy(t).start()
    for t in range(out_ref.shape[0]):
        copy(t).wait()


def order_tiles(held, owner, slot):
    count, (_, pieces, _, half, model) = owner.shape[0], held.shape
    scalar = pl.BlockSpec(memory_space=pltpu.SMEM)
    return pl.pallas_call(
        order_kernel,
        in_specs=[scalar, scalar, pl.BlockSpec(memory_space=pl.ANY)],
        out_specs=pl.BlockSpec(memory_space=pltpu.VMEM),
        out_shape=jax.ShapeDtypeStruct((count, pieces, half, model), bf16),
        scratch_shapes=[pltpu.SemaphoreType.DMA((count,))],
        compiler_params=pltpu.CompilerParams(vmem_limit_bytes=24 * 2**20),
        name="order_tiles",
    )(owner, slot, held)


def collect_kernel(count, owner_ref, slot_ref, *refs):
    sources, out_ref, sem = refs[:count], refs[-2], refs[-1]

    def copies():
        t = 0
        for source in sources:
            for i in range(source.shape[0]):
                yield pltpu.make_async_copy(source.at[i], out_ref.at[owner_ref[t], slot_ref[t]], sem.at[t])
                t += 1

    for copy in copies():
        copy.start()
    for copy in copies():
        copy.wait()


def collect(sources, owner, slot, n, slots, into=None):
    total, (half, model) = owner.shape[0], sources[0].shape[1:]
    scalar = pl.BlockSpec(memory_space=pltpu.SMEM)
    whole = pl.BlockSpec(memory_space=pltpu.VMEM)
    held = [] if into is None else [into]
    return pl.pallas_call(
        functools.partial(collect_kernel, len(sources)),
        in_specs=[scalar] * 2 + [whole] * len(sources) + [pl.BlockSpec(memory_space=pltpu.MemorySpace.HBM)] * len(held),
        out_specs=pl.BlockSpec(memory_space=pltpu.MemorySpace.HBM),
        out_shape=jax.ShapeDtypeStruct((n, slots, half, model), bf16),
        input_output_aliases={2 + len(sources): 0} if held else {},
        scratch_shapes=[pltpu.SemaphoreType.DMA((total,))],
        compiler_params=pltpu.CompilerParams(vmem_limit_bytes=58 * 2**20),
        name="collect",
    )(owner, slot, *sources, *held)


def attend_kernel(q_ref, *refs):
    kv_refs, (o_ref, total_ref) = refs[:-2], refs[-2:]
    scale = HEAD_DIM ** (-0.5)
    for i in range(q_ref.shape[0]):
        scores = [dot(kv[0, i], q_ref[i], ((0,), (0,))) * scale for kv in kv_refs]
        top = functools.reduce(jnp.maximum, [jnp.max(s, 0, keepdims=True) for s in scores])
        raised = [jnp.exp(s - top) for s in scores]
        total = sum(jnp.sum(e, 0, keepdims=True) for e in raised)
        share = 1.0 / total
        o_ref[i] = sum(
            dot(kv[1, i], (e * share).astype(bf16), ((1,), (0,))) for kv, e in zip(kv_refs, raised)
        ).astype(bf16)
        total_ref[i] = top + jnp.log(total)


def attend(queries, blocks):
    heads, size, rows = queries.shape
    step = 2
    short = pl.BlockSpec((step, size, rows), lambda h: (h, 0, 0))
    block = pl.BlockSpec((2, step, size, rows), lambda h: (0, h, 0, 0))
    return pl.pallas_call(
        attend_kernel,
        grid=(heads // step,),
        in_specs=[short] + [block] * len(blocks),
        out_specs=[short, pl.BlockSpec((step, 1, rows), lambda h: (h, 0, 0))],
        out_shape=[
            jax.ShapeDtypeStruct((heads, size, rows), bf16),
            jax.ShapeDtypeStruct((heads, 1, rows), f32),
        ],
        compiler_params=pltpu.CompilerParams(vmem_limit_bytes=32 * 2**20),
        name="attend",
    )(queries, *blocks)


def attend_back_kernel(count, q_ref, g_ref, total_ref, *refs):
    kv_refs, dq_ref, dkv_refs = refs[:count], refs[count], refs[count + 1:]
    scale = HEAD_DIM ** (-0.5)
    for i in range(q_ref.shape[0]):
        soft = [jnp.exp(dot(kv[0, i], q_ref[i], ((0,), (0,))) * scale - total_ref[i]) for kv in kv_refs]
        grad_soft = [dot(kv[1, i], g_ref[i], ((0,), (0,))) for kv in kv_refs]
        mean = sum(jnp.sum(p * g, 0, keepdims=True) for p, g in zip(soft, grad_soft))
        grad_scores = [(p * (g - mean)).astype(bf16) for p, g in zip(soft, grad_soft)]
        dq = sum(dot(kv[0, i], ds, ((1,), (0,))) for kv, ds in zip(kv_refs, grad_scores))
        dq_ref[i] = (dq * scale).astype(bf16)
        for dkv, p, ds in zip(dkv_refs, soft, grad_scores):
            dkv[0, i] = (dot(q_ref[i], ds, ((1,), (1,))) * scale).astype(bf16)
            dkv[1, i] = dot(g_ref[i], p.astype(bf16), ((1,), (1,))).astype(bf16)


def attend_back(queries, blocks, gradient, total):
    heads, size, rows = queries.shape
    step = 2
    short = pl.BlockSpec((step, size, rows), lambda h: (h, 0, 0))
    block = pl.BlockSpec((2, step, size, rows), lambda h: (0, h, 0, 0))
    return pl.pallas_call(
        functools.partial(attend_back_kernel, len(blocks)),
        grid=(heads // step,),
        in_specs=[short, short, pl.BlockSpec((step, 1, rows), lambda h: (h, 0, 0))] + [block] * len(blocks),
        out_specs=[short] + [block] * len(blocks),
        out_shape=[jax.ShapeDtypeStruct((heads, size, rows), bf16)]
        + [jax.ShapeDtypeStruct(kv.shape, bf16) for kv in blocks],
        compiler_params=pltpu.CompilerParams(vmem_limit_bytes=32 * 2**20),
        name="attend_back",
    )(queries, gradient, total, *blocks)


def adamw_update(weight, moment_one, moment_two, gradient, rate):
    moment_one = beta_first * moment_one + (1.0 - beta_first) * gradient
    moment_two = beta_second * moment_two + (1.0 - beta_second) * gradient * gradient
    first_hat = moment_one * (1.0 / (1.0 - beta_first**STEP))
    second_hat = moment_two * (1.0 / (1.0 - beta_second**STEP))
    weight = weight - rate * (first_hat / (jnp.sqrt(second_hat) + adam_eps) + weight_decay * weight)
    return (weight, moment_one, moment_two)


def tile_adamw_kernel(used_ref, core_ref, w_ref, m_ref, v_ref, own_ref, oth_ref, w_out, m_out, v_out):
    slot = pl.program_id(0)
    half = w_ref.shape[1] // 2

    @pl.when(used_ref[slot] == 1)
    def _():
        for h, g_ref in enumerate((own_ref, oth_ref)):
            side = core_ref[0] if h == 0 else 1 - core_ref[0]
            at = pl.ds(pl.multiple_of(side * half, half), half)
            new = adamw_update(w_ref[0, at], m_ref[0, at], v_ref[0, at], g_ref[0].astype(f32), learn_rate)
            w_out[0, at], m_out[0, at], v_out[0, at] = new

    @pl.when(used_ref[slot] != 1)
    def _():
        w_out[...], m_out[...], v_out[...] = w_ref[...], m_ref[...], v_ref[...]


def tile_adamw(used, core, state, own, oth):
    slots, rows, width = state[0].shape
    block = pl.BlockSpec((1, rows, width), lambda s, u, c: (s, 0, 0))
    grad_block = pl.BlockSpec((1, rows // 2, width), lambda s, u, c: (s, 0, 0))
    return pl.pallas_call(
        tile_adamw_kernel,
        grid_spec=pltpu.PrefetchScalarGridSpec(
            num_scalar_prefetch=2,
            grid=(slots,),
            in_specs=[block, block, block, grad_block, grad_block],
            out_specs=[block, block, block],
        ),
        out_shape=[jax.ShapeDtypeStruct(state[0].shape, f32)] * 3,
        compiler_params=pltpu.CompilerParams(vmem_limit_bytes=58 * 2**20),
        name="tile_adamw",
    )(used, core, *state, own, oth)


def body(
    token_ids,
    masked,
    tile_slot,
    tile_master,
    tile_first,
    tile_second,
    embedding,
    embed_first,
    embed_second,
    position_table,
    position_first,
    position_second,
    norm_params,
    norm_first,
    norm_second,
    head_bias,
    bias_first,
    bias_second,
):
    n = lax.axis_size("fsdp")
    z, core, ty, tx = (lax.axis_index(a) for a in EVERY)
    slots, width, model = tile_master.shape
    half = width // 2
    columns = 2 * width
    heads = columns // HEAD_DIM
    half_len = token_ids.shape[1]
    rows = half_len // 2
    share = rows // 2
    own_dim = embedding.shape[0]
    norms = norm_params.shape[1]
    core_arr = core.reshape(1).astype(jnp.int32)
    piece_at = core * 2 + ty

    owner = tile_slot // slots
    held = lax.dynamic_slice(tile_master, (0, core * half, 0), (slots, half, model)).astype(bf16)
    held = lax.all_gather(held, ("fsdp", "ctx", "ty"), axis=0, tiled=True).reshape(n, 4, slots, half, model)

    block_at, block = core * 2 + tx, 2 * BLOCK
    vocab_pad = 8 * BLOCK - VOCAB
    wide = block + rows
    embed_pad = jnp.pad(embedding.astype(bf16), ((0, 0), (0, vocab_pad)))
    ids_half = jnp.where(masked == 1, VOCAB - 1, token_ids)
    ids = lax.dynamic_slice(ids_half, (0, ty * rows), (1, rows))
    coded = lax.dynamic_slice(ids_half * 2 + masked, (0, ty * rows), (1, rows))
    coded = jnp.concatenate([coded // 256, coded % 256], 1).astype(bf16)
    packed = jnp.concatenate(
        [
            lax.dynamic_slice(embed_pad, (0, block_at * block), (own_dim, block)),
            lax.dynamic_slice(position_table, (0, piece_at * rows), (own_dim, rows)).astype(bf16),
        ],
        1,
    )
    packed = jnp.concatenate(
        [
            packed,
            jnp.pad(norm_params.astype(bf16).reshape(2 * norms, own_dim), ((0, 0), (0, wide - own_dim))),
            jnp.pad(coded, ((0, 15 - 2 * norms), (0, wide - 2 * rows))),
        ],
        0,
    )
    tables = lax.all_gather(packed, "fsdp", axis=0)
    embed_all = tables[:, :own_dim, :block].reshape(model, block)
    for axis, at in (("tx", tx), ("ctx", core)):
        embed_all = both(axis, embed_all, at, 1)
    places_own = tables[:, :own_dim, block:].reshape(model, rows).T.astype(f32)
    gains = tables[:, own_dim:own_dim + 2 * norms, :own_dim].transpose(1, 0, 2)
    gains = gains.reshape(2, norms, model).astype(f32)
    coded = tables[:, own_dim + 2 * norms, :2 * rows].reshape(n, 1, 2, rows)
    for axis, at in (("ty", ty), ("ctx", core)):
        coded = both(axis, coded, at, 1)
    coded = coded.astype(f32).astype(jnp.int32)
    coded = coded[:, :, 0] * 256 + coded[:, :, 1]
    all_ids = coded // 2
    count = jnp.sum(coded % 2).astype(f32)
    column_at = lax.broadcasted_iota(jnp.int32, (1, 8 * BLOCK), 1)
    pick_ids = (ids.reshape(rows, 1) == column_at).astype(bf16)
    stream = dot(pick_ids, embed_all, ((1,), (1,))) + places_own

    weights, kept_layers = [], []
    for layer in range(LAYERS):
        mine = slice(12 * layer, 12 * layer + 12)
        tiles = order_tiles(held, owner[mine], tile_slot[mine] % slots).reshape(12 * columns, model)
        w_qkv, w_o = tiles[:3 * columns], tiles[3 * columns:4 * columns]
        w_in, w_out = tiles[4 * columns:8 * columns], tiles[8 * columns:]
        weights.append((w_qkv, w_o, w_in, w_out))
        normed = norm_parts(stream, gains[0, 2 * layer], gains[1, 2 * layer])[0].astype(bf16)
        kv = dot(w_qkv[columns:], normed, ((1,), (1,))).astype(bf16)
        kv_y = over("ty", kv)
        blocks = [kv, kv_y, over("ctx", kv), over("ctx", kv_y)]
        blocks = [block.reshape(2, heads, HEAD_DIM, rows) for block in blocks]
        queries = dot(w_qkv[:columns], normed, ((1,), (1,))).astype(bf16).reshape(heads, HEAD_DIM, rows)
        mixed, log_total = attend(queries, blocks)
        mixed = mixed.reshape(columns, rows)
        middle = stream + sum_over_x(dot(mixed, w_o, ((0,), (0,))))
        normed_mlp = norm_parts(middle, gains[0, 2 * layer + 1], gains[1, 2 * layer + 1])[0].astype(bf16)
        pre_gelu = dot(normed_mlp, w_in, ((1,), (1,)))
        activation = jax.nn.gelu(pre_gelu, approximate=False).astype(bf16)
        kept_layers.append((stream, middle, queries, blocks, log_total, mixed, pre_gelu))
        stream = middle + sum_over_x(dot(activation, w_out, ((1,), (0,))))

    final_rows = lax.dynamic_slice_in_dim(stream, tx * share, share, 0)
    final_normed, hat_final, inv_final = norm_parts(final_rows, gains[0, 2 * LAYERS], gains[1, 2 * LAYERS])
    final_normed = final_normed.astype(bf16)
    bias_row = jnp.pad(head_bias, (0, vocab_pad)).reshape(1, 8 * BLOCK)
    logits = dot(final_normed, embed_all, ((1,), (0,))) + bias_row
    logits = jnp.where(column_at < VOCAB, logits, -1e30)
    start = ty * rows + tx * share
    targets = lax.dynamic_slice(token_ids, (0, start), (1, share)).reshape(share, 1)
    row_weights = lax.dynamic_slice(masked, (0, start), (1, share)).reshape(share, 1).astype(f32)
    row_top = jnp.max(logits, -1, keepdims=True)
    log_total = row_top + jnp.log(jnp.sum(jnp.exp(logits - row_top), -1, keepdims=True))
    is_target = targets == column_at
    picked = jnp.sum(jnp.where(is_target, logits, 0.0), -1, keepdims=True)
    loss_part = jnp.sum((log_total - picked) * row_weights)
    grad_logits = (
        (jnp.exp(logits - log_total) - is_target.astype(f32)) * (row_weights / count)
    ).astype(bf16)
    bias_sum = jnp.sum(grad_logits.astype(f32), 0, keepdims=True)
    bias_sum = jnp.where(column_at == 8 * BLOCK - 1, loss_part, bias_sum)
    for axis in PLANE:
        bias_sum = bias_sum + over(axis, bias_sum)
    bit = 1
    while bit < n:
        bias_sum = bias_sum + lax.ppermute(bias_sum, "fsdp", [(i, i ^ bit) for i in range(n)])
        bit *= 2
    bias_grad = bias_sum[0, :VOCAB]
    loss_value = bias_sum[0, 8 * BLOCK - 1] / count
    grad_final = dot(grad_logits, embed_all, ((1,), (1,)))
    part = norm_back(grad_final, hat_final, inv_final, gains[0, 2 * LAYERS]).astype(bf16)
    gradient = both("tx", part, tx, 0).astype(f32)
    final_norm_grad = jnp.stack([jnp.sum(grad_final * hat_final, 0), jnp.sum(grad_final, 0)])
    final_norm_grad = final_norm_grad + over("tx", final_norm_grad)

    embed_part = dot(final_normed, grad_logits, ((0,), (0,))).astype(bf16)
    embed_part = lax.psum_scatter(embed_part, "fsdp", scatter_dimension=0, tiled=True)
    offloaded = [embed_part]
    for axis, at in (("ctx", core), ("tx", tx), ("ty", ty)):
        cut = embed_part.shape[1] // 2
        keep = lax.dynamic_slice_in_dim(embed_part, at * cut, cut, 1)
        send = lax.dynamic_slice_in_dim(embed_part, cut - at * cut, cut, 1)
        embed_part = add_halves(keep, over(axis, send))
    embed_head = embed_part
    for axis, at in (("ty", ty), ("tx", tx), ("ctx", core)):
        embed_head = both(axis, embed_head, at, 1)

    norm_grads = [None] * norms
    norm_grads[2 * LAYERS] = final_norm_grad
    tile_grads, tile_list = [], []

    def core_sum(grads):
        keep = lax.dynamic_slice_in_dim(grads, core * 2, 2, 1).astype(bf16)
        send = lax.dynamic_slice_in_dim(grads, 2 - core * 2, 2, 1).astype(bf16)
        return add_halves(keep, over("ctx", send)).transpose(1, 0, 2, 3)

    def neighbour_sum(two):
        keep = lax.dynamic_index_in_dim(two, ty, 0, False)
        send = lax.dynamic_index_in_dim(two, 1 - ty, 0, False)
        return add_halves(keep, over("ty", send))

    def offloaded_sum(flat, axis):
        flat = after(flat, offloaded[0]) if len(offloaded) == 1 else flat
        offloaded.append(lax.psum_scatter(flat, axis, scatter_dimension=0, tiled=True))
        return offloaded[-1]

    attn_two = None
    for layer in reversed(range(LAYERS)):
        stream, middle, queries, blocks, log_total, mixed, pre_gelu = kept_layers[layer]
        w_qkv, w_o, w_in, w_out = weights[layer]
        branch = gradient.astype(bf16)
        activation = jax.nn.gelu(pre_gelu, approximate=False).astype(bf16)
        grad_act = dot(branch, w_out, ((1,), (1,)))
        grad_pre = (grad_act * gelu_slope(pre_gelu)).astype(bf16)
        normed_mlp, hat_mlp, inv_mlp = norm_parts(middle, gains[0, 2 * layer + 1], gains[1, 2 * layer + 1])
        partial = dot(grad_pre, w_in, ((1,), (0,))).astype(bf16)
        grad_normed = sum_over_x(partial)
        grad_out = dot(needs(activation, partial), branch, ((0,), (0,))).reshape(4, 4, half, model)
        grad_in = dot(grad_pre, needs(normed_mlp.astype(bf16), partial), ((0,), (0,))).reshape(4, 4, half, model)
        two = core_sum(jnp.concatenate([grad_in, grad_out], 0))
        tile_list += range(12 * layer + 4, 12 * layer + 12)
        if attn_two is not None:
            two = jnp.concatenate([two, attn_two], 1)
            tile_list += range(12 * layer + 12, 12 * layer + 16)
        grad_middle = gradient + norm_back(grad_normed, hat_mlp, inv_mlp, gains[0, 2 * layer + 1])
        norm_grads[2 * layer + 1] = jnp.stack([jnp.sum(grad_normed * hat_mlp, 0), jnp.sum(grad_normed, 0)])
        branch = grad_middle.astype(bf16)
        grad_proj_out = dot(mixed, branch, ((1,), (0,)))
        grad_mixed = dot(w_o, branch, ((1,), (1,))).astype(bf16).reshape(heads, HEAD_DIM, rows)
        grad_queries, kv_own, kv_y, kv_core, kv_both = attend_back(queries, blocks, grad_mixed, log_total)
        kv_own = kv_own.astype(f32) + over("ctx", kv_core).astype(f32)
        from_y = over("ty", add_halves(kv_y, over("ctx", kv_both)))
        grad_kv = (kv_own + from_y.astype(f32)).astype(bf16).reshape(2 * columns, rows)
        two = needs(two, from_y) if layer else two
        tile_grads.append(offloaded_sum(two.reshape(-1, half, model), "ty"))
        grad_qkv = jnp.concatenate([grad_queries.reshape(columns, rows), grad_kv], 0)
        normed, hat_attn, inv_attn = norm_parts(stream, gains[0, 2 * layer], gains[1, 2 * layer])
        partial = dot(grad_qkv, w_qkv, ((0,), (0,))).astype(bf16)
        grad_normed = sum_over_x(partial)
        grad_w = dot(grad_qkv, needs(normed.astype(bf16), partial), ((1,), (0,)))
        grad_w = jnp.concatenate([grad_w, grad_proj_out], 0).reshape(4, 4, half, model)
        attn_two = core_sum(grad_w)
        gradient = grad_middle + norm_back(grad_normed, hat_attn, inv_attn, gains[0, 2 * layer])
        norm_grads[2 * layer] = jnp.stack([jnp.sum(grad_normed * hat_attn, 0), jnp.sum(grad_normed, 0)])

    norm_rows = jnp.stack(norm_grads, 1).reshape(2 * norms, model)
    state = jnp.concatenate(
        [gradient.astype(bf16), norm_rows.astype(bf16), jnp.zeros((16 - 2 * norms, model), bf16)], 0
    )
    state = state.reshape(rows + 16, n, own_dim).transpose(1, 0, 2)
    state = lax.all_to_all(state, "fsdp", 0, 0)[:, None]
    last_grads = needs(neighbour_sum(attn_two), state)
    state = both("ty", state, ty, 1)
    state = both("ctx", state, core, 1)
    norm_grad = jnp.sum(state[:, :, rows:rows + 2 * norms].astype(f32), (0, 1)).reshape(2, norms, own_dim)
    token_grads = state[:, :, :rows]
    position_grad = jnp.sum(token_grads.astype(f32), 0).reshape(4 * rows, own_dim).T
    picks = (all_ids.reshape(n * 4 * rows, 1) == column_at).astype(bf16)
    embed_tail = dot(token_grads.reshape(n * 4 * rows, own_dim), picks, ((0,), (0,)))
    embed_grad = (embed_tail + embed_head.astype(f32))[:, :VOCAB]

    at = jnp.array(tile_list, jnp.int32)
    sent = collect(tile_grads, owner[at], tile_slot[at] % slots, n, slots)
    sent = collect([last_grads], owner[:4], tile_slot[:4] % slots, n, slots, sent)
    tile_sum = offloaded_sum(sent.reshape(-1, half, model), "fsdp")
    used = jnp.any((tile_slot - z * slots)[None, :] == jnp.arange(slots, dtype=jnp.int32)[:, None], 1).astype(jnp.int32)
    state = (tile_master, tile_first, tile_second)
    embed_upd = adamw_update(embedding, embed_first, embed_second, embed_grad, learn_rate)
    position_upd = adamw_update(position_table, position_first, position_second, position_grad, learn_rate)
    norm_upd = adamw_update(norm_params, norm_first, norm_second, norm_grad, small_rate)
    bias_upd = adamw_update(head_bias, bias_first, bias_second, bias_grad, small_rate)
    tile_sum = after(tile_sum, (embed_upd, position_upd, norm_upd, bias_upd, loss_value))
    tile_upd = tile_adamw(used, core_arr, state, tile_sum, over("ctx", tile_sum))
    return (loss_value, *tile_upd, *embed_upd, *position_upd, *norm_upd, *bias_upd)


def solution(mesh):
    grid = Mesh(mesh.devices.reshape(-1, 2, 2, 2), EVERY)
    halves, tiles, table = P("fsdp", "ctx"), P("fsdp", ("ty", "tx"), None), P("fsdp", None)
    norms, copied = P(None, None, "fsdp"), P()

    def three(spec):
        return (spec,) * 3

    return jax.shard_map(
        body,
        mesh=grid,
        in_specs=(halves, halves, copied, *three(tiles), *three(table), *three(table), *three(norms), *three(copied)),
        out_specs=(copied, *three(tiles), *three(table), *three(table), *three(norms), *three(copied)),
        check_vma=False,
    )
```
